128 devices in a mesh: dp: 8 (over z, y_lo), fsdp: 16 (over y_hi, x, core).
Axes of the slice: x: 4, y: 4 (y_hi: 2, y_lo: 2; y = y_hi * 2 + y_lo), z: 4, core: 2. Of those that a mesh axis runs over, the one named last changes fastest.
Arguments:
- hidden: bfloat16 [2048, 32, 5120], P(('dp', 'fsdp')), may hold values from -6 to 6
- queries: bfloat16 [2048, 32, 2560], P(('dp', 'fsdp')), may hold values from -6 to 6
- out_grad: bfloat16 [2048, 32, 2560], P(('dp', 'fsdp')), may hold values from -6 to 6
- counts: int32 [2048], P(('dp', 'fsdp')), may hold values from 1 to 2
- send_peer: int32 [2048], P(('dp', 'fsdp')), may hold values from 0 to 7, as said below
- recv_from: int32 [2048], P(('dp', 'fsdp')), may hold values from 0 to 7, as said below
- key_weight: bfloat16 [5120, 512], P('fsdp'), may hold values from -0.6 to 0.6
- value_weight: bfloat16 [5120, 512], P('fsdp'), may hold values from -0.078125 to 0.078125
Outputs:
- hidden_grad: bfloat16 [2048, 32, 5120], P(('dp', 'fsdp'))
- key_grad: float32 [5120, 512], P('fsdp')
- value_grad: float32 [5120, 512], P('fsdp')
The draws below stay inside these ranges and needn't reach their ends.
Inputs may be any that keep to these rules, and one draw needn't show every extreme that they name: Within each fsdp index, every device sends 8 - 1 trajectories, one to each other dp index, and receives one from each; a slot whose send_peer is its own dp index is kept, and an arriving trajectory fills a slot whose recv_from names its sender. recv_from is the inverse of send_peer in the sense above: slot s of device (a, b) with recv_from = c != a receives the unique slot of device (c, b) whose send_peer is a.
All inputs are finite; a program needn't handle non-finite values.
Results may differ from the reference program's by a relative error of at most 0.025.
Values may be sent and summed in bfloat16 or wider, within the bound.
A program may use at most 192 MiB of HBM per device.

```python
import jax
import jax.numpy as jnp
from jax import lax

D = 5120
HD = 128
KVH = 4
GROUP = 5
QW = 2560
KVW = 512
JBLK = 16
MAXIT = 2
TLEN = 32
SLOTS = 16
TOTAL_SLOTS = 2048
N_DP = 8
N_FSDP = 16


def routing_tables(key):
    shift_keys = jax.random.split(jax.random.fold_in(key, 101), N_FSDP)
    distances = jnp.arange(1, N_DP, dtype=jnp.int32)
    shifts = jax.vmap(lambda one_key: jax.random.permutation(one_key, distances))(shift_keys)
    slot_keys = jax.random.split(jax.random.fold_in(key, 202), N_DP * N_FSDP)
    orders = jax.vmap(lambda one_key: jax.random.permutation(one_key, SLOTS))(slot_keys).reshape(N_DP, N_FSDP, SLOTS)
    ranking = jnp.argsort(orders, axis=-1).astype(jnp.int32)
    movers = N_DP - 1
    spread_shifts = jnp.broadcast_to(shifts[None, :, :], (N_DP, N_FSDP, movers))
    picked = jnp.take_along_axis(spread_shifts, jnp.clip(ranking, 0, movers - 1), axis=-1)
    moving = ranking < movers
    home_group = jnp.arange(N_DP, dtype=jnp.int32)[:, None, None]
    sending = jnp.where(moving, (home_group + picked) % N_DP, home_group)
    arriving = jnp.where(moving, (home_group - picked) % N_DP, home_group)
    return (sending.reshape(-1).astype(jnp.int32), arriving.reshape(-1).astype(jnp.int32))


def draw_send_peer(key, part):
    tables = routing_tables(key)
    return tables[0]


def draw_recv_from(key, part):
    tables = routing_tables(key)
    return tables[1]


def draw_hidden(key, part):
    key = jax.random.fold_in(key, 11)
    shape = (TOTAL_SLOTS, TLEN, D)
    return jnp.clip(jax.random.normal(key, shape, jnp.float32), -6.0, 6.0).astype(jnp.bfloat16)


def draw_queries(key, part):
    key = jax.random.fold_in(key, 12)
    shape = (TOTAL_SLOTS, TLEN, QW)
    return jnp.clip(jax.random.normal(key, shape, jnp.float32), -6.0, 6.0).astype(jnp.bfloat16)


def draw_key_weight(key, part):
    key = jax.random.fold_in(key, 13)
    return (jnp.clip(jax.random.normal(key, (D, KVW), jnp.float32), -6.0, 6.0) * D ** (-0.5)).astype(jnp.bfloat16)


def set_ends(entries, rng, least, high):
    extent = entries.shape
    spot = [jax.random.randint(jax.random.fold_in(rng, axis), (), 0, extent[axis]) for axis in range(len(extent))]
    entries = entries.at[tuple(spot)].set(least)
    longest = extent.index(max(extent))
    spot[longest] = (spot[longest] + 1) % extent[longest]
    return entries.at[tuple(spot)].set(high)


def levels(own_key, dims, cuts, least, high):
    factor_of, own = 1.0, jax.random.fold_in(own_key, 6)
    for axis_at, parts in cuts:
        heights = jnp.exp(jax.random.uniform(jax.random.fold_in(own, axis_at), (parts,), jnp.float32, least / len(cuts), high / len(cuts)))
        factor_of = factor_of * jnp.repeat(heights, dims[axis_at] // parts).reshape([-1 if axis == axis_at else 1 for axis in range(len(dims))])
    return factor_of


def bell_draw(rng, shape, spread, limit, pieces=(), kind=jnp.bfloat16):
    values = spread * jax.random.normal(rng, shape, jnp.float32)
    if pieces:
        values = values * levels(rng, shape, pieces, -0.22, 0.18)
    return jnp.clip(values, -limit, limit).astype(kind)


def setup_inputs(seed: int = 0) -> dict:
    key_of = jax.random.split(jax.random.key(seed), 9)
    hidden = draw_hidden(jax.random.fold_in(key_of[8], 71), 0)
    queries = draw_queries(jax.random.fold_in(key_of[8], 71), 0)
    out_grad = bell_draw(key_of[2], (TOTAL_SLOTS, TLEN, QW), 1.0, 6.0, ((0, 128),))
    counts = set_ends(jax.random.randint(key_of[3], (TOTAL_SLOTS,), 1, MAXIT + 1), jax.random.fold_in(key_of[3], 1), 1, MAXIT).astype(jnp.int32)
    send_peer = draw_send_peer(jax.random.fold_in(key_of[8], 71), 0)
    recv_from = draw_recv_from(jax.random.fold_in(key_of[8], 71), 0)
    key_weight = draw_key_weight(jax.random.fold_in(key_of[8], 71), 0)
    value_weight = bell_draw(key_of[7], (D, KVW), D ** -0.5, 0.078125, ((0, 16),))
    return dict(hidden=hidden, queries=queries, out_grad=out_grad, counts=counts, send_peer=send_peer, recv_from=recv_from, key_weight=key_weight, value_weight=value_weight)


def attention_backward(hidden_rows, query_rows, grad_rows, slot_counts, key_weight, value_weight):
    flat_rows = hidden_rows.reshape(SLOTS * TLEN, D)
    key_rows = jnp.dot(flat_rows, key_weight, preferred_element_type=jnp.float32).astype(jnp.bfloat16)
    value_rows = jnp.dot(flat_rows, value_weight, preferred_element_type=jnp.float32).astype(jnp.bfloat16)
    keys_wide = key_rows.astype(jnp.float32).reshape(SLOTS, TLEN, KVH, HD)
    values_wide = value_rows.astype(jnp.float32).reshape(SLOTS, TLEN, KVH, HD)
    query_wide = query_rows.astype(jnp.float32).reshape(SLOTS, TLEN, KVH, GROUP, HD)
    score_scale = HD ** -0.5
    scores = jnp.einsum("stgrd,sugd->sgrtu", query_wide, keys_wide) * score_scale
    positions = jnp.arange(TLEN, dtype=jnp.int32)
    live_rows = positions[None, :] < (slot_counts * JBLK)[:, None]
    allowed = (positions[:, None] >= positions[None, :])[None, :, :] & live_rows[:, None, :]
    allowed = allowed[:, None, None, :, :]
    scores = jnp.where(allowed, scores, -1e30)
    top_score = jnp.max(scores, axis=-1, keepdims=True)
    exponent_terms = jnp.exp(scores - top_score)
    probs = exponent_terms / jnp.sum(exponent_terms, axis=-1, keepdims=True)
    probs_half = probs.astype(jnp.bfloat16)
    attended = jnp.einsum("sgrtu,sugd->stgrd", probs_half.astype(jnp.float32), values_wide)
    row_weight = live_rows.astype(jnp.float32) / slot_counts.astype(jnp.float32)[:, None]
    out_delta = (grad_rows.astype(jnp.float32).reshape(SLOTS, TLEN, KVH, GROUP, HD) * row_weight[:, :, None, None, None]).astype(jnp.bfloat16)
    delta_wide = out_delta.astype(jnp.float32)
    value_delta = jnp.einsum("sgrtu,stgrd->sugd", probs_half.astype(jnp.float32), delta_wide).astype(jnp.bfloat16)
    prob_delta = jnp.einsum("stgrd,sugd->sgrtu", delta_wide, values_wide)
    row_delta = jnp.einsum("stgrd,stgrd->sgrt", delta_wide, attended)
    score_delta = (probs * (prob_delta - row_delta[..., None]) * score_scale).astype(jnp.bfloat16)
    key_delta = jnp.einsum("sgrtu,stgrd->sugd", score_delta.astype(jnp.float32), query_wide).astype(jnp.bfloat16)
    key_flat = key_delta.reshape(SLOTS * TLEN, KVW)
    value_flat = value_delta.reshape(SLOTS * TLEN, KVW)
    hidden_delta = jnp.dot(key_flat, key_weight.T, preferred_element_type=jnp.float32) + jnp.dot(value_flat, value_weight.T, preferred_element_type=jnp.float32)
    pair_delta = jnp.concatenate([key_flat, value_flat], axis=1)
    device_term = jnp.dot(flat_rows.T, pair_delta, preferred_element_type=jnp.float32)
    return hidden_delta.astype(jnp.bfloat16).reshape(SLOTS, TLEN, D), device_term


def reference(hidden, queries, out_grad, counts, send_peer, recv_from, key_weight, value_weight):
    devices_all = N_DP * N_FSDP
    grid_shape = (N_DP, N_FSDP, SLOTS)
    hidden_all = hidden.reshape(N_DP, N_FSDP, SLOTS, TLEN, D)
    query_all = queries.reshape(N_DP, N_FSDP, SLOTS, TLEN, QW)
    grad_all = out_grad.reshape(N_DP, N_FSDP, SLOTS, TLEN, QW)
    count_all = counts.reshape(grid_shape)
    sends = send_peer.reshape(grid_shape)
    sources = recv_from.reshape(grid_shape)
    home_group = jnp.arange(N_DP, dtype=jnp.int32)[:, None, None]
    column_ids = jnp.arange(N_FSDP, dtype=jnp.int32)[None, :, None]
    source_sends = sends[sources, column_ids]
    matched = source_sends == home_group[..., None]
    slot_ids = jnp.arange(SLOTS, dtype=jnp.int32)
    found_slot = jnp.sum(jnp.where(matched, slot_ids, 0), axis=-1).astype(jnp.int32)
    source_slot = jnp.where(sources == home_group, slot_ids[None, None, :], found_slot).astype(jnp.int32)

    def device_step(total, index):
        group_id = index // N_FSDP
        member_id = index % N_FSDP
        rows_from = sources[group_id, member_id]
        slots_from = source_slot[group_id, member_id]
        hidden_rows = hidden_all[rows_from, member_id, slots_from]
        query_rows = query_all[rows_from, member_id, slots_from]
        grad_rows = grad_all[rows_from, member_id, slots_from]
        slot_counts = count_all[rows_from, member_id, slots_from]
        hidden_delta, device_term = attention_backward(hidden_rows, query_rows, grad_rows, slot_counts, key_weight, value_weight)
        return total + device_term, hidden_delta

    total, hidden_grads = lax.scan(device_step, jnp.zeros((D, 2 * KVW), jnp.float32), jnp.arange(devices_all, dtype=jnp.int32))
    return hidden_grads.reshape(devices_all * SLOTS, TLEN, D), total[:, :KVW], total[:, KVW:]
```

```python
import jax
import jax.numpy as jnp
from jax import lax
from jax.sharding import PartitionSpec as P

HD = 128
JBLK = 16


def attention_backward(hidden_rows, query_rows, grad_rows, slot_counts, key_full, value_full):
    slot_total, token_slots, width = hidden_rows.shape
    head_size = HD
    kv_heads = key_full.shape[1] // head_size
    flat_rows = hidden_rows.reshape(slot_total * token_slots, width)
    key_rows = jnp.dot(flat_rows, key_full, preferred_element_type=jnp.float32).astype(jnp.bfloat16)
    value_rows = jnp.dot(flat_rows, value_full, preferred_element_type=jnp.float32).astype(
        jnp.bfloat16
    )
    keys_split = key_rows.reshape(slot_total, token_slots, kv_heads, head_size)
    values_split = value_rows.reshape(slot_total, token_slots, kv_heads, head_size)
    query_split = query_rows.reshape(slot_total, token_slots, kv_heads, -1, head_size)
    score_scale = head_size ** (-0.5)
    scores = (
        jnp.einsum("stgrd,sugd->sgrtu", query_split, keys_split, preferred_element_type=jnp.float32)
        * score_scale
    )
    positions = jnp.arange(token_slots, dtype=jnp.float32)
    live_rows = positions[None, :] < (slot_counts * JBLK)[:, None]
    allowed = (positions[:, None] >= positions[None, :])[None, :, :] & live_rows[:, None, :]
    allowed = allowed[:, None, None, :, :]
    scores = jnp.where(allowed, scores, -1e30)
    top_score = jnp.max(scores, axis=-1, keepdims=True)
    exponent_terms = jnp.exp(scores - top_score)
    probs = exponent_terms / jnp.sum(exponent_terms, axis=-1, keepdims=True)
    probs_half = probs.astype(jnp.bfloat16)
    attended = jnp.einsum(
        "sgrtu,sugd->stgrd", probs_half, values_split, preferred_element_type=jnp.float32
    )
    row_weight = live_rows.astype(jnp.float32) / slot_counts[:, None]
    grad_split = grad_rows.reshape(slot_total, token_slots, kv_heads, -1, head_size)
    out_delta = (grad_split * row_weight[:, :, None, None, None]).astype(jnp.bfloat16)
    value_delta = jnp.einsum(
        "sgrtu,stgrd->sugd", probs_half, out_delta, preferred_element_type=jnp.float32
    ).astype(jnp.bfloat16)
    prob_delta = jnp.einsum(
        "stgrd,sugd->sgrtu", out_delta, values_split, preferred_element_type=jnp.float32
    )
    row_delta = jnp.sum(out_delta.astype(jnp.float32) * attended, axis=-1)
    row_delta = jnp.transpose(row_delta, (0, 2, 3, 1))
    score_delta = (probs * (prob_delta - row_delta[..., None]) * score_scale).astype(jnp.bfloat16)
    key_delta = jnp.einsum(
        "sgrtu,stgrd->sugd", score_delta, query_split, preferred_element_type=jnp.float32
    ).astype(jnp.bfloat16)
    key_flat = key_delta.reshape(slot_total * token_slots, -1)
    value_flat = value_delta.reshape(slot_total * token_slots, -1)
    return (flat_rows, key_flat, value_flat)


def block_plan(send_peer, recv_from, own_group, group_count):
    peer_ids = jnp.arange(group_count, dtype=jnp.int32)
    staying = recv_from == own_group
    chosen = ((send_peer[None, :] == peer_ids[:, None]) & (peer_ids[:, None] != own_group)).astype(
        jnp.bfloat16
    )
    placing = (
        (recv_from[:, None] == peer_ids[None, :]) & jnp.logical_not(staying)[:, None]
    ).astype(jnp.bfloat16)
    return (chosen, placing, staying)


def select_rows(chosen, source):
    return jnp.einsum("ps,stf->ptf", chosen, source, preferred_element_type=jnp.float32).astype(
        jnp.bfloat16
    )


def settle(own_rows, incoming, placing, staying):
    arrived_rows = jnp.einsum(
        "sp,ptf->stf", placing, incoming, preferred_element_type=jnp.float32
    ).astype(jnp.bfloat16)
    return jnp.where(staying[:, None, None], own_rows, arrived_rows)


def body(hidden, queries, out_grad, counts, send_peer, recv_from, key_weight, value_weight):
    width = key_weight.shape[1]
    pair_full = lax.all_gather(
        jnp.concatenate([key_weight, value_weight], axis=1), "fsdp", axis=0, tiled=True
    )
    key_full, value_full = pair_full[:, :width], pair_full[:, width:]
    group_count = lax.axis_size("dp")
    own_group = lax.axis_index("dp")
    chosen, placing, staying = block_plan(send_peer, recv_from, own_group, group_count)
    flat_rows, key_flat, value_flat = attention_backward(
        hidden, queries, out_grad, counts.astype(jnp.float32), key_full, value_full
    )
    pair_delta = jnp.concatenate([key_flat, value_flat], axis=1)
    slots, tokens = hidden.shape[0], hidden.shape[1]
    pair_rows = pair_delta.reshape(slots, tokens, 2 * width)
    arrived = lax.all_to_all(
        select_rows(chosen, pair_rows), "dp", split_axis=0, concat_axis=0, tiled=True
    )
    partial_rows = lax.psum_scatter(
        jnp.einsum("rd,rk->dk", flat_rows, pair_delta, preferred_element_type=jnp.float32).astype(
            jnp.bfloat16
        ),
        "fsdp",
        scatter_dimension=0,
        tiled=True,
    )
    settled = settle(pair_rows, arrived, placing, staying).reshape(slots * tokens, 2 * width)
    hidden_grad = (
        jnp.einsum("rk,dk->rd", settled, pair_full, preferred_element_type=jnp.float32)
        .astype(jnp.bfloat16)
        .reshape(hidden.shape)
    )
    weight_grad = lax.psum(partial_rows, "dp").astype(jnp.float32)
    return (hidden_grad, weight_grad[:, :width], weight_grad[:, width:])


def solution(mesh):
    return jax.shard_map(
        body,
        mesh=mesh,
        in_specs=(
            P(("dp", "fsdp"), None, None),
            P(("dp", "fsdp"), None, None),
            P(("dp", "fsdp"), None, None),
            P(("dp", "fsdp")),
            P(("dp", "fsdp")),
            P(("dp", "fsdp")),
            P("fsdp", None),
            P("fsdp", None),
        ),
        out_specs=(P(("dp", "fsdp"), None, None), P("fsdp", None), P("fsdp", None)),
        check_vma=False,
    )
```

```python
import jax
import jax.numpy as jnp
from jax import lax
from jax.experimental import pallas as pl
from jax.experimental.pallas import tpu as pltpu
from jax.sharding import PartitionSpec as P

HD = 128
JBLK = 16
WIDE = 384
MESH = pl.DeviceIdType.MESH


def place():
    d, f = lax.axis_index("dp"), lax.axis_index("fsdp")
    return lax.rem(lax.div(f, 2), 4), lax.div(f, 8), lax.rem(d, 2), lax.div(d, 2), lax.rem(f, 2)


def device(x, h, l, z, c):
    return (z * 2 + l, (h * 4 + x) * 2 + c)


def gather_kernel(hidden, kw, vw, pair_out, w_out, w, hid, send_sem, recv_sem, local_sem):
    x, h, l, z, c = place()
    rows, width = kw.shape
    cols = 2 * width
    quarter = rows // 4

    def wrap(v):
        return lax.rem(v + 4, 4)

    xp, xm = device(wrap(x + 1), h, l, z, c), device(wrap(x - 1), h, l, z, c)
    zp, zm = device(x, h, l, wrap(z + 1), c), device(x, h, l, wrap(z - 1), c)
    yo, peer = device(x, 1 - h, 1 - l, z, c), device(x, h, l, z, 1 - c)

    hid_copy = pltpu.make_async_copy(hidden, hid, local_sem.at[0])
    hid_copy.start()
    own = (h * 4 + x) * 2 + c
    w[own, :, pl.ds(0, width)] = kw[...]
    w[own, :, pl.ds(width, width)] = vw[...]

    barrier = pltpu.get_barrier_semaphore()
    for other in (xp, xm, zp, zm, yo, peer):
        pl.semaphore_signal(barrier, inc=1, device_id=other, device_id_type=MESH)
    pl.semaphore_wait(barrier, 6)

    number = {}
    started = []

    def copy(name, f, row, col, target):
        i = number.setdefault(name, len(number))
        ref = w.at[f, pl.ds(*row), pl.ds(*col)]
        return pltpu.make_async_remote_copy(
            src_ref=ref, dst_ref=ref, send_sem=send_sem.at[i], recv_sem=recv_sem.at[i],
            device_id=target, device_id_type=MESH,
        )

    def send(name, f, row, col, target):
        one = copy(name, f, row, col, target)
        one.start()
        started.append(one)

    def arrive(name, f, row, col):
        copy(name, f, row, col, peer).wait_recv()

    def block(hh, dx, core=c):
        return (hh * 4 + wrap(x + dx)) * 2 + core

    def part(dz):
        return (pl.multiple_of(wrap(z + dz) * quarter, quarter), quarter)

    def halves(odd):
        first = 256 if odd else 384
        return (WIDE, first), (WIDE + first, cols - WIDE - first)

    side = (h, 1 - h)
    narrow, wide = (WIDE, cols - WIDE), (0, WIDE)
    whole, low, high = (0, rows), (0, rows // 2), (rows // 2, rows // 2)

    send("cy", own, part(0), narrow, yo)
    send("cxp0", own, part(0), narrow, xp)
    send("cxm0", own, part(0), narrow, xm)
    send("own", own, whole, (0, cols), peer)

    def along_z(b, f):
        send(f"zp{b}", f, part(0), narrow, zp)
        send(f"zm{b}", f, part(0), narrow, zm)

    order = [(1, 0), (0, -1), (0, 1), (1, -1), (1, 1), (0, 2), (1, 2)]
    arrive("cy", block(side[1], 0), part(0), narrow)
    send("cxp1", block(side[1], 0), part(0), narrow, xp)
    send("cxm1", block(side[1], 0), part(0), narrow, xm)
    along_z(0, block(side[1], 0))
    for s in (0, 1):
        one, two = halves(s)
        arrive(f"cxp{s}", block(side[s], -1), part(0), narrow)
        send(f"cfp{s}", block(side[s], -1), part(0), one, xp)
        along_z(1 + 2 * s, block(side[s], -1))
        arrive(f"cxm{s}", block(side[s], 1), part(0), narrow)
        send(f"cfm{s}", block(side[s], 1), part(0), two, xm)
        along_z(2 + 2 * s, block(side[s], 1))
    send("ay", own, whole, wide, yo)
    send("axp0", own, whole, wide, xp)
    send("axm0", own, whole, wide, xm)
    for s in (0, 1):
        one, two = halves(s)
        arrive(f"cfp{s}", block(side[s], 2), part(0), one)
        arrive(f"cfm{s}", block(side[s], 2), part(0), two)
        along_z(5 + s, block(side[s], 2))

    def forward_z(b):
        s, dx = order[b]
        one, two = halves(b % 2)
        f = block(side[s], dx)
        arrive(f"zp{b}", f, part(-1), narrow)
        send(f"zfp{b}", f, part(-1), one, zp)
        arrive(f"zm{b}", f, part(1), narrow)
        send(f"zfm{b}", f, part(1), two, zm)

    def finish_z(b):
        s, dx = order[b]
        one, two = halves(b % 2)
        f = block(side[s], dx)
        arrive(f"zfp{b}", f, part(2), one)
        arrive(f"zfm{b}", f, part(2), two)
        send(f"pc{b}", f, whole, narrow, peer)

    def forward_x(s):
        arrive(f"axp{s}", block(side[s], -1), whole, wide)
        send(f"afp{s}", block(side[s], -1), low, wide, xp)
        arrive(f"axm{s}", block(side[s], 1), whole, wide)
        send(f"afm{s}", block(side[s], 1), high, wide, xm)
        send(f"pa{1 + 2 * s}", block(side[s], -1), whole, wide, peer)
        send(f"pa{2 + 2 * s}", block(side[s], 1), whole, wide, peer)

    forward_z(0)
    forward_z(1)
    arrive("ay", block(side[1], 0), whole, wide)
    send("axp1", block(side[1], 0), whole, wide, xp)
    send("axm1", block(side[1], 0), whole, wide, xm)
    send("pa0", block(side[1], 0), whole, wide, peer)
    forward_z(2)
    forward_z(3)
    forward_x(0)
    forward_z(4)
    forward_z(5)
    finish_z(0)
    finish_z(1)
    forward_z(6)
    forward_x(1)
    for b in range(2, 6):
        finish_z(b)
    for s in (0, 1):
        arrive(f"afp{s}", block(side[s], 2), low, wide)
        arrive(f"afm{s}", block(side[s], 2), high, wide)
        send(f"pa{5 + s}", block(side[s], 2), whole, wide, peer)
    finish_z(6)
    arrive("own", block(side[0], 0, 1 - c), whole, (0, cols))
    for b in range(7):
        s, dx = order[b]
        arrive(f"pa{b}", block(side[s], dx, 1 - c), whole, wide)
        arrive(f"pc{b}", block(side[s], dx, 1 - c), whole, narrow)
    w_copy = pltpu.make_async_copy(w, w_out, local_sem.at[1])
    w_copy.start()
    hid_copy.wait()

    blocks = w.shape[0]
    tokens = hidden.shape[0] * hidden.shape[1]
    group = 4

    @pl.loop(0, cols // 256)
    def _(n):
        at = pl.ds(pl.multiple_of(n * 256, 256), 256)
        total = jnp.zeros((tokens, 256), jnp.float32)
        for k in range(blocks // group):
            left = hid[:, :, pl.ds(k * group * rows, group * rows)].reshape(tokens, group * rows)
            right = w[pl.ds(k * group, group), :, at].reshape(group * rows, 256)
            total = total + jnp.dot(left, right, preferred_element_type=jnp.float32)
        pair_out[:, at] = total.astype(jnp.bfloat16)

    w_copy.wait()
    for one in started:
        one.wait_send()


def gather_project(hidden, key_weight, value_weight):
    rows, width = key_weight.shape
    tokens = hidden.shape[0] * hidden.shape[1]
    blocks = lax.axis_size("fsdp")
    vmem = pl.BlockSpec(memory_space=pltpu.VMEM)
    hbm = pl.BlockSpec(memory_space=pl.ANY)
    return pl.pallas_call(
        gather_kernel,
        name="gather_project",
        out_shape=(
            jax.ShapeDtypeStruct((tokens, 2 * width), jnp.bfloat16),
            jax.ShapeDtypeStruct((blocks, rows, 2 * width), jnp.bfloat16),
        ),
        in_specs=[hbm, vmem, vmem],
        out_specs=(vmem, hbm),
        scratch_shapes=[
            pltpu.VMEM((blocks, rows, 2 * width), jnp.bfloat16),
            pltpu.VMEM(hidden.shape, jnp.bfloat16),
            pltpu.SemaphoreType.DMA((64,)),
            pltpu.SemaphoreType.DMA((64,)),
            pltpu.SemaphoreType.DMA((2,)),
        ],
        compiler_params=pltpu.CompilerParams(
            collective_id=0, has_side_effects=True, vmem_limit_bytes=48 << 20
        ),
        cost_estimate=pl.CostEstimate(
            flops=2 * tokens * blocks * rows * 2 * width, bytes_accessed=22 << 20, transcendentals=0
        ),
    )(hidden, key_weight, value_weight)


def attention_backward(hidden_rows, query_rows, grad_rows, slot_counts, key_rows, value_rows):
    slot_total, token_slots, width = hidden_rows.shape
    head_size = HD
    kv_heads = key_rows.shape[1] // head_size
    flat_rows = hidden_rows.reshape(slot_total * token_slots, width)
    keys_split = key_rows.reshape(slot_total, token_slots, kv_heads, head_size)
    values_split = value_rows.reshape(slot_total, token_slots, kv_heads, head_size)
    query_split = query_rows.reshape(slot_total, token_slots, kv_heads, -1, head_size)
    score_scale = head_size ** (-0.5)
    scores = (
        jnp.einsum("stgrd,sugd->sgrtu", query_split, keys_split, preferred_element_type=jnp.float32)
        * score_scale
    )
    positions = jnp.arange(token_slots, dtype=jnp.float32)
    live_rows = positions[None, :] < (slot_counts * JBLK)[:, None]
    allowed = (positions[:, None] >= positions[None, :])[None, :, :] & live_rows[:, None, :]
    allowed = allowed[:, None, None, :, :]
    scores = jnp.where(allowed, scores, -1e30)
    top_score = jnp.max(scores, axis=-1, keepdims=True)
    exponent_terms = jnp.exp(scores - top_score)
    probs = exponent_terms / jnp.sum(exponent_terms, axis=-1, keepdims=True)
    probs_half = probs.astype(jnp.bfloat16)
    attended = jnp.einsum(
        "sgrtu,sugd->stgrd", probs_half, values_split, preferred_element_type=jnp.float32
    )
    row_weight = live_rows.astype(jnp.float32) / slot_counts[:, None]
    grad_split = grad_rows.reshape(slot_total, token_slots, kv_heads, -1, head_size)
    out_delta = (grad_split * row_weight[:, :, None, None, None]).astype(jnp.bfloat16)
    value_delta = jnp.einsum(
        "sgrtu,stgrd->sugd", probs_half, out_delta, preferred_element_type=jnp.float32
    ).astype(jnp.bfloat16)
    prob_delta = jnp.einsum(
        "stgrd,sugd->sgrtu", out_delta, values_split, preferred_element_type=jnp.float32
    )
    row_delta = jnp.sum(out_delta.astype(jnp.float32) * attended, axis=-1)
    row_delta = jnp.transpose(row_delta, (0, 2, 3, 1))
    score_delta = (probs * (prob_delta - row_delta[..., None]) * score_scale).astype(jnp.bfloat16)
    key_delta = jnp.einsum(
        "sgrtu,stgrd->sugd", score_delta, query_split, preferred_element_type=jnp.float32
    ).astype(jnp.bfloat16)
    key_flat = key_delta.reshape(slot_total * token_slots, -1)
    value_flat = value_delta.reshape(slot_total * token_slots, -1)
    return (flat_rows, key_flat, value_flat)


def block_plan(send_peer, recv_from, own_group, group_count):
    peer_ids = jnp.arange(group_count, dtype=jnp.int32)
    staying = recv_from == own_group
    chosen = ((send_peer[None, :] == peer_ids[:, None]) & (peer_ids[:, None] != own_group)).astype(
        jnp.bfloat16
    )
    placing = (
        (recv_from[:, None] == peer_ids[None, :]) & jnp.logical_not(staying)[:, None]
    ).astype(jnp.bfloat16)
    return (chosen, placing, staying)


def select_rows(chosen, source):
    return jnp.einsum("ps,stf->ptf", chosen, source, preferred_element_type=jnp.float32).astype(
        jnp.bfloat16
    )


def settle(own_rows, incoming, placing, staying):
    arrived_rows = jnp.einsum(
        "sp,ptf->stf", placing, incoming, preferred_element_type=jnp.float32
    ).astype(jnp.bfloat16)
    return jnp.where(staying[:, None, None], own_rows, arrived_rows)


def body(hidden, queries, out_grad, counts, send_peer, recv_from, key_weight, value_weight):
    width = key_weight.shape[1]
    pair, w_blocks = gather_project(hidden, key_weight, value_weight)
    pair_full = w_blocks.reshape(-1, 2 * width)
    group_count = lax.axis_size("dp")
    own_group = lax.axis_index("dp")
    chosen, placing, staying = block_plan(send_peer, recv_from, own_group, group_count)
    flat_rows, key_flat, value_flat = attention_backward(
        hidden, queries, out_grad, counts.astype(jnp.float32), pair[:, :width], pair[:, width:]
    )
    pair_delta = jnp.concatenate([key_flat, value_flat], axis=1)
    slots, tokens = hidden.shape[0], hidden.shape[1]
    pair_rows = pair_delta.reshape(slots, tokens, 2 * width)
    arrived = lax.all_to_all(
        select_rows(chosen, pair_rows), "dp", split_axis=0, concat_axis=0, tiled=True
    )
    partial_rows = lax.psum_scatter(
        jnp.einsum("rd,rk->dk", flat_rows, pair_delta, preferred_element_type=jnp.float32).astype(
            jnp.bfloat16
        ),
        "fsdp",
        scatter_dimension=0,
        tiled=True,
    )
    settled = settle(pair_rows, arrived, placing, staying).reshape(slots * tokens, 2 * width)
    hidden_grad = (
        jnp.einsum("rk,dk->rd", settled, pair_full, preferred_element_type=jnp.float32)
        .astype(jnp.bfloat16)
        .reshape(hidden.shape)
    )
    weight_grad = lax.psum(partial_rows, "dp").astype(jnp.float32)
    return (hidden_grad, weight_grad[:, :width], weight_grad[:, width:])


def solution(mesh):
    return jax.shard_map(
        body,
        mesh=mesh,
        in_specs=(
            P(("dp", "fsdp"), None, None),
            P(("dp", "fsdp"), None, None),
            P(("dp", "fsdp"), None, None),
            P(("dp", "fsdp")),
            P(("dp", "fsdp")),
            P(("dp", "fsdp")),
            P("fsdp", None),
            P("fsdp", None),
        ),
        out_specs=(P(("dp", "fsdp"), None, None), P("fsdp", None), P("fsdp", None)),
        check_vma=False,
    )
```

```python
import jax
import jax.numpy as jnp
from jax import lax
from jax.experimental import pallas as pl
from jax.experimental.pallas import tpu as pltpu
from jax.sharding import PartitionSpec as P

HD = 128
JBLK = 16
WIDE = 384
MESH = pl.DeviceIdType.MESH


def place():
    d, f = lax.axis_index("dp"), lax.axis_index("fsdp")
    return lax.rem(lax.div(f, 2), 4), lax.div(f, 8), lax.rem(d, 2), lax.div(d, 2), lax.rem(f, 2)


def device(x, h, l, z, c):
    return (z * 2 + l, (h * 4 + x) * 2 + c)


def gather_kernel(hidden, kw, vw, pair_out, w_out, w, hid, send_sem, recv_sem, local_sem):
    x, h, l, z, c = place()
    rows, width = kw.shape
    cols = 2 * width
    quarter = rows // 4

    def wrap(v):
        return lax.rem(v + 4, 4)

    xp, xm = device(wrap(x + 1), h, l, z, c), device(wrap(x - 1), h, l, z, c)
    zp, zm = device(x, h, l, wrap(z + 1), c), device(x, h, l, wrap(z - 1), c)
    yo, peer = device(x, 1 - h, 1 - l, z, c), device(x, h, l, z, 1 - c)

    hid_copy = pltpu.make_async_copy(hidden, hid, local_sem.at[0])
    hid_copy.start()
    own = (h * 4 + x) * 2 + c
    w[own, :, pl.ds(0, width)] = kw[...]
    w[own, :, pl.ds(width, width)] = vw[...]

    barrier = pltpu.get_barrier_semaphore()
    for other in (xp, xm, zp, zm, yo, peer):
        pl.semaphore_signal(barrier, inc=1, device_id=other, device_id_type=MESH)
    pl.semaphore_wait(barrier, 6)

    number = {}
    started = []

    def copy(name, f, row, col, target):
        i = number.setdefault(name, len(number))
        ref = w.at[f, pl.ds(*row), pl.ds(*col)]
        return pltpu.make_async_remote_copy(
            src_ref=ref, dst_ref=ref, send_sem=send_sem.at[i], recv_sem=recv_sem.at[i],
            device_id=target, device_id_type=MESH,
        )

    def send(name, f, row, col, target):
        one = copy(name, f, row, col, target)
        one.start()
        started.append(one)

    def arrive(name, f, row, col):
        copy(name, f, row, col, peer).wait_recv()

    def block(hh, dx, core=c):
        return (hh * 4 + wrap(x + dx)) * 2 + core

    def part(dz):
        return (pl.multiple_of(wrap(z + dz) * quarter, quarter), quarter)

    def halves(odd):
        first = 256 if odd else 384
        return (WIDE, first), (WIDE + first, cols - WIDE - first)

    side = (h, 1 - h)
    narrow, wide = (WIDE, cols - WIDE), (0, WIDE)
    whole, low, high = (0, rows), (0, rows // 2), (rows // 2, rows // 2)

    send("cy", own, part(0), narrow, yo)
    send("cxp0", own, part(0), narrow, xp)
    send("cxm0", own, part(0), narrow, xm)
    send("own", own, whole, (0, cols), peer)

    def along_z(b, f):
        send(f"zp{b}", f, part(0), narrow, zp)
        send(f"zm{b}", f, part(0), narrow, zm)

    order = [(1, 0), (0, -1), (0, 1), (1, -1), (1, 1), (0, 2), (1, 2)]
    arrive("cy", block(side[1], 0), part(0), narrow)
    send("cxp1", block(side[1], 0), part(0), narrow, xp)
    send("cxm1", block(side[1], 0), part(0), narrow, xm)
    along_z(0, block(side[1], 0))
    for s in (0, 1):
        one, two = halves(s)
        arrive(f"cxp{s}", block(side[s], -1), part(0), narrow)
        send(f"cfp{s}", block(side[s], -1), part(0), one, xp)
        along_z(1 + 2 * s, block(side[s], -1))
        arrive(f"cxm{s}", block(side[s], 1), part(0), narrow)
        send(f"cfm{s}", block(side[s], 1), part(0), two, xm)
        along_z(2 + 2 * s, block(side[s], 1))
    send("ay", own, whole, wide, yo)
    send("axp0", own, whole, wide, xp)
    send("axm0", own, whole, wide, xm)
    for s in (0, 1):
        one, two = halves(s)
        arrive(f"cfp{s}", block(side[s], 2), part(0), one)
        arrive(f"cfm{s}", block(side[s], 2), part(0), two)
        along_z(5 + s, block(side[s], 2))

    def forward_z(b):
        s, dx = order[b]
        one, two = halves(b % 2)
        f = block(side[s], dx)
        arrive(f"zp{b}", f, part(-1), narrow)
        send(f"zfp{b}", f, part(-1), one, zp)
        arrive(f"zm{b}", f, part(1), narrow)
        send(f"zfm{b}", f, part(1), two, zm)

    def finish_z(b):
        s, dx = order[b]
        one, two = halves(b % 2)
        f = block(side[s], dx)
        arrive(f"zfp{b}", f, part(2), one)
        arrive(f"zfm{b}", f, part(2), two)
        send(f"pc{b}", f, whole, narrow, peer)

    def forward_x(s):
        arrive(f"axp{s}", block(side[s], -1), whole, wide)
        send(f"afp{s}", block(side[s], -1), low, wide, xp)
        arrive(f"axm{s}", block(side[s], 1), whole, wide)
        send(f"afm{s}", block(side[s], 1), high, wide, xm)
        send(f"pa{1 + 2 * s}", block(side[s], -1), whole, wide, peer)
        send(f"pa{2 + 2 * s}", block(side[s], 1), whole, wide, peer)

    forward_z(0)
    forward_z(1)
    arrive("ay", block(side[1], 0), whole, wide)
    send("axp1", block(side[1], 0), whole, wide, xp)
    send("axm1", block(side[1], 0), whole, wide, xm)
    send("pa0", block(side[1], 0), whole, wide, peer)
    forward_z(2)
    forward_z(3)
    forward_x(0)
    forward_z(4)
    forward_z(5)
    finish_z(0)
    finish_z(1)
    forward_z(6)
    forward_x(1)
    for b in range(2, 6):
        finish_z(b)
    for s in (0, 1):
        arrive(f"afp{s}", block(side[s], 2), low, wide)
        arrive(f"afm{s}", block(side[s], 2), high, wide)
        send(f"pa{5 + s}", block(side[s], 2), whole, wide, peer)
    finish_z(6)
    arrive("own", block(side[0], 0, 1 - c), whole, (0, cols))
    for b in range(7):
        s, dx = order[b]
        arrive(f"pa{b}", block(side[s], dx, 1 - c), whole, wide)
        arrive(f"pc{b}", block(side[s], dx, 1 - c), whole, narrow)
    w_copy = pltpu.make_async_copy(w, w_out, local_sem.at[1])
    w_copy.start()
    hid_copy.wait()

    blocks = w.shape[0]
    tokens = hidden.shape[0] * hidden.shape[1]
    group = 4

    @pl.loop(0, cols // 256)
    def _(n):
        at = pl.ds(pl.multiple_of(n * 256, 256), 256)
        total = jnp.zeros((tokens, 256), jnp.float32)
        for k in range(blocks // group):
            left = hid[:, :, pl.ds(k * group * rows, group * rows)].reshape(tokens, group * rows)
            right = w[pl.ds(k * group, group), :, at].reshape(group * rows, 256)
            total = total + jnp.dot(left, right, preferred_element_type=jnp.float32)
        pair_out[:, at] = total.astype(jnp.bfloat16)

    w_copy.wait()
    for one in started:
        one.wait_send()


def gather_project(hidden, key_weight, value_weight):
    rows, width = key_weight.shape
    tokens = hidden.shape[0] * hidden.shape[1]
    blocks = lax.axis_size("fsdp")
    vmem = pl.BlockSpec(memory_space=pltpu.VMEM)
    hbm = pl.BlockSpec(memory_space=pl.ANY)
    return pl.pallas_call(
        gather_kernel,
        name="gather_project",
        out_shape=(
            jax.ShapeDtypeStruct((tokens, 2 * width), jnp.bfloat16),
            jax.ShapeDtypeStruct((blocks, rows, 2 * width), jnp.bfloat16),
        ),
        in_specs=[hbm, vmem, vmem],
        out_specs=(vmem, hbm),
        scratch_shapes=[
            pltpu.VMEM((blocks, rows, 2 * width), jnp.bfloat16),
            pltpu.VMEM(hidden.shape, jnp.bfloat16),
            pltpu.SemaphoreType.DMA((64,)),
            pltpu.SemaphoreType.DMA((64,)),
            pltpu.SemaphoreType.DMA((2,)),
        ],
        compiler_params=pltpu.CompilerParams(
            collective_id=0, has_side_effects=True, vmem_limit_bytes=48 << 20
        ),
        cost_estimate=pl.CostEstimate(
            flops=2 * tokens * blocks * rows * 2 * width, bytes_accessed=22 << 20, transcendentals=0
        ),
    )(hidden, key_weight, value_weight)


def reduce_kernel(
    recv, pair, leaving, hidden, w_in, hg_out, gt_out,
    hid, w, dt, arrived, settled, hgb, summed, give, take,
    p0_half, p0_last, p1_half, p1_last, p2_half, p2_last,
    p0_two, p1_two, p2_two, p0_three, p1_three, p2_three, done,
    send_sem, recv_sem, local_sem,
):
    x, h, l, z, c = place()
    me = lax.axis_index("dp")
    y = 2 * h + l
    half = dt.shape[1]
    span = summed.shape[2]
    slots, tokens, _ = hidden.shape
    total = slots * tokens
    f32, bf16 = jnp.float32, jnp.bfloat16

    def wrap(v):
        return lax.rem(v + 4, 4)

    def at(dx=0, dy=0, dz=0, core=c):
        q = wrap(y + dy)
        return device(wrap(x + dx), lax.div(q, 2), lax.rem(q, 2), wrap(z + dz), core)

    xp, xm, x2 = at(dx=1), at(dx=-1), at(dx=2)
    yp, ym, y2 = at(dy=1), at(dy=-1), at(dy=2)
    zp, zm, z2 = at(dz=1), at(dz=-1), at(dz=2)
    peer = at(core=1 - c)
    twin = device(x, h, 1 - l, z, c)
    group = lax.axis_size("dp")
    f = lax.axis_index("fsdp")

    hid_copy = pltpu.make_async_copy(hidden, hid, local_sem.at[0])
    hid_copy.start()
    w_copy = pltpu.make_async_copy(w_in, w, local_sem.at[1])
    w_copy.start()

    others = [(lax.rem(me + j, group), f) for j in range(1, group)]
    others += [xp, xm, x2, device(x, 1 - h, 1 - l, z, c), y2, peer]
    barrier = pltpu.get_barrier_semaphore()
    for other in others:
        pl.semaphore_signal(barrier, inc=1, device_id=other, device_id_type=MESH)
    pl.semaphore_wait(barrier, len(others))

    number = {}
    started = []

    def copy(name, src, dst, target):
        i = number.setdefault(name, len(number))
        return pltpu.make_async_remote_copy(
            src_ref=src, dst_ref=dst, send_sem=send_sem.at[i], recv_sem=recv_sem.at[i],
            device_id=target, device_id_type=MESH,
        )

    def send(name, src, dst, target):
        one = copy(name, src, dst, target)
        one.start()
        started.append(one)

    def arrive(name, dst):
        copy(name, dst, dst, peer).wait_recv()

    def add(*refs):
        value = refs[0][...].astype(f32)
        for ref in refs[1:]:
            value = value + ref[...].astype(f32)
        return value.astype(bf16)

    arrived[me] = jnp.zeros(arrived.shape[1:], bf16)
    for j in range(1, group):
        to = lax.rem(me + j, group)
        send(f"a{j}", leaving.at[to], arrived.at[me], (to, f))
    for t in (0, 1):
        dt[t] = pair[:, t * half : (t + 1) * half].T

    lanes = (pl.ds(0, 256), pl.ds(256, 256), pl.ds(512, 128))
    order = [(0, 2), (1, 2), (1, 1), (0, -1), (0, 1), (1, -1), (0, 0), (1, 0)]

    def index(hh, dx):
        return hh * 4 + wrap(x + dx)

    def term(t, k):
        cols = pl.ds(pl.multiple_of(k * span, 128), span)
        return jnp.dot(dt[t], hid[:, :, cols].reshape(total, span), preferred_element_type=f32)

    def other_half(i):
        k = index(*order[i])
        give[k] = term(1 - c, k).astype(bf16)
        send(f"d{i}", give.at[k], take.at[k], peer)

    def own_half(i):
        k = index(*order[i])
        value = term(c, k)
        arrive(f"d{i}", take.at[k])
        summed[k] = (value + take[k].astype(f32)).astype(bf16)

    def zrows(dz):
        return pl.ds(pl.multiple_of(wrap(z + dz) * 128, 128), 128)

    def part1_first(i):
        k = index(*order[i])
        up, down = (2, -1) if i % 2 == 0 else (1, 2)
        one, two = ("h", "n") if i % 2 == 0 else ("n", "h")
        far_dst, near_dst = p1_half.at[i], p1_last.at[1 if i % 2 == 0 else 0, i]
        dst = {"h": far_dst, "n": near_dst}
        send(f"z{one}{i}", summed.at[k, zrows(up), lanes[1]], dst[one], zp)
        send(f"z{two}{i}", summed.at[k, zrows(down), lanes[1]], dst[two], zm)

    def part1_second(i):
        k = index(*order[i])
        near, target = (1, zp) if i % 2 == 0 else (-1, zm)
        arrive(f"zh{i}", p1_half.at[i])
        ref = summed.at[k, zrows(near), lanes[1]]
        ref[...] = add(ref, p1_half.at[i])
        send(f"zl{i}", ref, p1_last.at[0 if i % 2 == 0 else 1, i], target)

    def part1_last(i):
        k = index(*order[i])
        arrive(f"zn{i}", p1_last.at[1 if i % 2 == 0 else 0, i])
        arrive(f"zl{i}", p1_last.at[0 if i % 2 == 0 else 1, i])
        ref = summed.at[k, zrows(0), lanes[1]]
        ref[...] = add(ref, p1_last.at[0, i], p1_last.at[1, i])

    def yref(dy, dx):
        q = wrap(y + dy)
        rows = pl.ds(pl.multiple_of(lax.rem(q, 2) * 256, 256), 256)
        return summed.at[lax.div(q, 2) * 4 + wrap(x + dx), rows, lanes[2]]

    shifts = (2, 1, -1, 0)

    def part2_first(j):
        dx = shifts[j]
        if j % 2 == 0:
            send(f"yh{j}", yref(2, dx), p2_half.at[j], yp)
            send(f"yn{j}", yref(-1, dx), p2_last.at[1, j], ym)
        else:
            send(f"yn{j}", yref(1, dx), p2_last.at[0, j], yp)
            send(f"yh{j}", yref(2, dx), p2_half.at[j], ym)

    def part2_second(j):
        near, target = (1, yp) if j % 2 == 0 else (-1, ym)
        arrive(f"yh{j}", p2_half.at[j])
        ref = yref(near, shifts[j])
        ref[...] = add(ref, p2_half.at[j])
        send(f"yl{j}", ref, p2_last.at[0 if j % 2 == 0 else 1, j], target)

    def part2_last(j):
        arrive(f"yn{j}", p2_last.at[1 if j % 2 == 0 else 0, j])
        arrive(f"yl{j}", p2_last.at[0 if j % 2 == 0 else 1, j])
        ref = yref(0, shifts[j])
        ref[...] = add(ref, p2_last.at[0, j], p2_last.at[1, j])

    def xref(hh, dx):
        return summed.at[index(hh, dx), :, lanes[0]]

    hid_copy.wait()
    other_half(0)
    other_half(1)
    for i in range(8):
        own_half(i)
        if i == 0:
            send("xh0", xref(0, 2), p0_half.at[0], xp)
        elif i == 1:
            send("xh1", xref(1, 2), p0_half.at[1], xm)
        elif i == 2:
            send("xn1", xref(1, 1), p0_last.at[0, 1], xp)
        elif i == 3:
            send("xn0", xref(0, -1), p0_last.at[1, 0], xm)
        part1_first(i)
        if i == 1:
            part2_first(0)
        elif i == 5:
            part2_first(1)
            part2_first(2)
        elif i == 7:
            part2_first(3)
        if i + 2 < 8:
            other_half(i + 2)
        if i >= 3:
            part1_second(i - 3)
        if i == 5:
            part2_second(0)
    arrive("xh0", p0_half.at[0])
    xref(0, 1)[...] = add(xref(0, 1), p0_half.at[0])
    send("xl0", xref(0, 1), p0_last.at[0, 0], xp)
    arrive("xh1", p0_half.at[1])
    xref(1, -1)[...] = add(xref(1, -1), p0_half.at[1])
    send("xl1", xref(1, -1), p0_last.at[1, 1], xm)
    part1_second(5)
    part2_second(1)
    part2_second(2)

    for j in range(1, group):
        arrive(f"a{j}", arrived.at[lax.rem(me + group - j, group)])
    for s in range(slots):
        source = recv[s]
        kept = pair[pl.ds(s * tokens, tokens), :]
        settled[pl.ds(s * tokens, tokens), :] = jnp.where(source == me, kept, arrived[source])
    w_copy.wait()
    hg_copies = []

    def back(j):
        block = w[2 * j : 2 * j + 2].reshape(span, w.shape[2])
        value = lax.dot_general(
            settled[...], block, (((1,), (1,)), ((), ())), preferred_element_type=f32
        )
        cols = pl.ds(j * span, span)
        hgb[:, :, cols] = value.astype(bf16).reshape(slots, tokens, span)
        one = pltpu.make_async_copy(hgb.at[:, :, cols], hg_out.at[:, :, cols], local_sem.at[2 + j])
        one.start()
        hg_copies.append(one)

    back(0)
    part1_second(6)
    back(1)
    part2_second(3)
    part1_second(7)
    for i in range(4):
        part1_last(i)
    back(2)
    part2_last(0)
    part1_last(4)
    part1_last(5)
    back(3)
    part2_last(1)
    part2_last(2)
    back(4)
    part2_last(3)
    part1_last(6)
    part1_last(7)

    steps = ((1, xp), (-1, xm), (2, x2))
    for n, (dx, target) in enumerate(steps):
        for hh in (0, 1):
            src = summed.at[index(hh, dx), zrows(0), lanes[1]]
            send(f"s1{n}{hh}", src, p1_two.at[n, hh], target)

    def zpiece(dz):
        rows = pl.ds(pl.multiple_of(l * 256 + wrap(z + dz) * 64, 64), 64)
        return summed.at[pl.ds(pl.multiple_of(h * 4, 4), 4), rows, lanes[2]]

    for n, (dz, target) in enumerate(((1, zp), (-1, zm), (2, z2))):
        send(f"s2{n}", zpiece(dz), p2_two.at[n], target)
    for hh in (0, 1):
        arrive(f"xn{hh}", p0_last.at[1 - hh, hh])
        arrive(f"xl{hh}", p0_last.at[hh, hh])
        xref(hh, 0)[...] = add(xref(hh, 0), p0_last.at[0, hh], p0_last.at[1, hh])

    def ypiece(dy):
        q = wrap(y + dy)
        rows = pl.ds(pl.multiple_of(lax.rem(q, 2) * 256, 256), 256)
        return summed.at[lax.div(q, 2) * 4 + x, rows, lanes[0]]

    for n, (dy, target) in enumerate(((1, yp), (-1, ym), (2, y2))):
        send(f"s0{n}", ypiece(dy), p0_two.at[n], target)
    back(5)
    for n in range(3):
        arrive(f"s2{n}", p2_two.at[n])
    zpiece(0)[...] = add(zpiece(0), p2_two.at[0], p2_two.at[1], p2_two.at[2])

    piece_rows = pl.ds(pl.multiple_of(l * 256 + z * 64, 64), 64)
    for n, (dx, target) in enumerate(steps):
        send(f"t2{n}", summed.at[index(h, dx), piece_rows, lanes[2]], p2_three.at[n], target)
    back(6)
    for n in range(3):
        for hh in (0, 1):
            arrive(f"s1{n}{hh}", p1_two.at[n, hh])
    for hh in (0, 1):
        ref = summed.at[index(hh, 0), zrows(0), lanes[1]]
        ref[...] = add(ref, p1_two.at[0, hh], p1_two.at[1, hh], p1_two.at[2, hh])

    def third1(dy):
        q = wrap(y + dy)
        rows = pl.ds(pl.multiple_of(z * 128 + lax.rem(q, 2) * 64, 64), 64)
        return summed.at[lax.div(q, 2) * 4 + x, rows, lanes[1]]

    for n, (dy, target) in enumerate(((1, yp), (-1, ym), (2, y2))):
        send(f"t1{n}", third1(dy), p1_three.at[n], target)
    back(7)
    for n in range(3):
        arrive(f"s0{n}", p0_two.at[n])
    ypiece(0)[...] = add(ypiece(0), p0_two.at[0], p0_two.at[1], p0_two.at[2])

    def third0(dz):
        rows = pl.ds(pl.multiple_of(l * 256 + wrap(z + dz) * 64, 64), 64)
        return summed.at[h * 4 + x, rows, lanes[0]]

    for n, (dz, target) in enumerate(((1, zp), (-1, zm), (2, z2))):
        send(f"t0{n}", third0(dz), p0_three.at[n], target)

    def finish(part, ref, buffer):
        for n in range(3):
            arrive(f"t{part}{n}", buffer.at[n])
        value = add(ref, buffer.at[0], buffer.at[1], buffer.at[2])
        mine = done.at[c, l, z, :, lanes[part]]
        mine[...] = value
        send(f"gy{part}", mine, mine, twin)
        send(f"gp{part}", mine, mine, zp)
        send(f"gm{part}", mine, mine, zm)
        send(f"g2{part}", mine, mine, z2)

    def pass_on(part):
        def piece(ll, dz):
            return done.at[c, ll, wrap(z + dz), :, lanes[part]]

        arrive(f"gy{part}", piece(1 - l, 0))
        send(f"fp{part}", piece(1 - l, 0), piece(1 - l, 0), zp)
        send(f"fm{part}", piece(1 - l, 0), piece(1 - l, 0), zm)
        arrive(f"g2{part}", piece(l, 2))
        send(f"fy{part}", piece(l, 2), piece(l, 2), twin)

    def collect(part):
        def piece(ll, dz):
            return done.at[c, ll, wrap(z + dz), :, lanes[part]]

        arrive(f"gp{part}", piece(l, -1))
        arrive(f"gm{part}", piece(l, 1))
        arrive(f"fp{part}", piece(1 - l, -1))
        arrive(f"fm{part}", piece(1 - l, 1))
        arrive(f"fy{part}", piece(1 - l, 2))
        ref = done.at[c, :, :, :, lanes[part]]
        send(f"e{part}", ref, ref, peer)

    finish(2, summed.at[h * 4 + x, piece_rows, lanes[2]], p2_three)
    finish(1, third1(0), p1_three)
    pass_on(2)
    finish(0, third0(0), p0_three)
    pass_on(1)
    collect(2)
    pass_on(0)
    collect(1)
    collect(0)
    for part in (2, 1, 0):
        arrive(f"e{part}", done.at[1 - c, :, :, :, lanes[part]])
    out_copy = pltpu.make_async_copy(done, gt_out, local_sem.at[10])
    out_copy.start()
    for one in started:
        one.wait_send()
    for one in hg_copies:
        one.wait()
    out_copy.wait()


def reduce_back(recv_from, pair, leaving, hidden, w_blocks):
    blocks, rows, cols = w_blocks.shape
    half, span = cols // 2, 2 * rows
    chips = blocks // 2
    total = pair.shape[0]
    bf16 = jnp.bfloat16
    vmem = pl.BlockSpec(memory_space=pltpu.VMEM)
    hbm = pl.BlockSpec(memory_space=pl.ANY)
    buffer = lambda *shape: pltpu.VMEM(shape, bf16)
    return pl.pallas_call(
        reduce_kernel,
        name="reduce_back",
        out_shape=(
            jax.ShapeDtypeStruct(hidden.shape, bf16),
            jax.ShapeDtypeStruct((2, 2, 4, half // 8, span), bf16),
        ),
        in_specs=[pl.BlockSpec(memory_space=pltpu.SMEM), vmem, vmem, hbm, hbm],
        out_specs=(hbm, hbm),
        scratch_shapes=[
            buffer(*hidden.shape),
            buffer(blocks, rows, cols),
            buffer(2, half, total),
            buffer(*leaving.shape),
            buffer(total, cols),
            buffer(*hidden.shape),
            buffer(chips, half, span),
            buffer(chips, half, span),
            buffer(chips, half, span),
            buffer(2, half, 256),
            buffer(2, 2, half, 256),
            buffer(8, half // 4, 256),
            buffer(2, 8, half // 4, 256),
            buffer(4, half // 2, 128),
            buffer(2, 4, half // 2, 128),
            buffer(3, half // 2, 256),
            buffer(3, 2, half // 4, 256),
            buffer(3, 4, half // 8, 128),
            buffer(3, half // 8, 256),
            buffer(3, half // 8, 256),
            buffer(3, half // 8, 128),
            buffer(2, 2, 4, half // 8, span),
            pltpu.SemaphoreType.DMA((112,)),
            pltpu.SemaphoreType.DMA((112,)),
            pltpu.SemaphoreType.DMA((11,)),
        ],
        compiler_params=pltpu.CompilerParams(
            collective_id=1, has_side_effects=True, vmem_limit_bytes=60 << 20
        ),
        cost_estimate=pl.CostEstimate(
            flops=4 * total * blocks * rows * cols, bytes_accessed=22 << 20, transcendentals=0
        ),
    )(recv_from, pair, leaving, hidden, w_blocks)


def attention_backward(hidden_rows, query_rows, grad_rows, slot_counts, key_rows, value_rows):
    slot_total, token_slots, width = hidden_rows.shape
    head_size = HD
    kv_heads = key_rows.shape[1] // head_size
    flat_rows = hidden_rows.reshape(slot_total * token_slots, width)
    keys_split = key_rows.reshape(slot_total, token_slots, kv_heads, head_size)
    values_split = value_rows.reshape(slot_total, token_slots, kv_heads, head_size)
    query_split = query_rows.reshape(slot_total, token_slots, kv_heads, -1, head_size)
    score_scale = head_size ** (-0.5)
    scores = (
        jnp.einsum("stgrd,sugd->sgrtu", query_split, keys_split, preferred_element_type=jnp.float32)
        * score_scale
    )
    positions = jnp.arange(token_slots, dtype=jnp.float32)
    live_rows = positions[None, :] < (slot_counts * JBLK)[:, None]
    allowed = (positions[:, None] >= positions[None, :])[None, :, :] & live_rows[:, None, :]
    allowed = allowed[:, None, None, :, :]
    scores = jnp.where(allowed, scores, -1e30)
    top_score = jnp.max(scores, axis=-1, keepdims=True)
    exponent_terms = jnp.exp(scores - top_score)
    probs = exponent_terms / jnp.sum(exponent_terms, axis=-1, keepdims=True)
    probs_half = probs.astype(jnp.bfloat16)
    attended = jnp.einsum(
        "sgrtu,sugd->stgrd", probs_half, values_split, preferred_element_type=jnp.float32
    )
    row_weight = live_rows.astype(jnp.float32) / slot_counts[:, None]
    grad_split = grad_rows.reshape(slot_total, token_slots, kv_heads, -1, head_size)
    out_delta = (grad_split * row_weight[:, :, None, None, None]).astype(jnp.bfloat16)
    value_delta = jnp.einsum(
        "sgrtu,stgrd->sugd", probs_half, out_delta, preferred_element_type=jnp.float32
    ).astype(jnp.bfloat16)
    prob_delta = jnp.einsum(
        "stgrd,sugd->sgrtu", out_delta, values_split, preferred_element_type=jnp.float32
    )
    row_delta = jnp.sum(out_delta.astype(jnp.float32) * attended, axis=-1)
    row_delta = jnp.transpose(row_delta, (0, 2, 3, 1))
    score_delta = (probs * (prob_delta - row_delta[..., None]) * score_scale).astype(jnp.bfloat16)
    key_delta = jnp.einsum(
        "sgrtu,stgrd->sugd", score_delta, query_split, preferred_element_type=jnp.float32
    ).astype(jnp.bfloat16)
    key_flat = key_delta.reshape(slot_total * token_slots, -1)
    value_flat = value_delta.reshape(slot_total * token_slots, -1)
    return (flat_rows, key_flat, value_flat)


def block_plan(send_peer, recv_from, own_group, group_count):
    peer_ids = jnp.arange(group_count, dtype=jnp.int32)
    staying = recv_from == own_group
    chosen = ((send_peer[None, :] == peer_ids[:, None]) & (peer_ids[:, None] != own_group)).astype(
        jnp.bfloat16
    )
    placing = (
        (recv_from[:, None] == peer_ids[None, :]) & jnp.logical_not(staying)[:, None]
    ).astype(jnp.bfloat16)
    return (chosen, placing, staying)


def select_rows(chosen, source):
    return jnp.einsum("ps,stf->ptf", chosen, source, preferred_element_type=jnp.float32).astype(
        jnp.bfloat16
    )


def body(hidden, queries, out_grad, counts, send_peer, recv_from, key_weight, value_weight):
    width = key_weight.shape[1]
    pair, w_blocks = gather_project(hidden, key_weight, value_weight)
    group_count = lax.axis_size("dp")
    own_group = lax.axis_index("dp")
    chosen, placing, staying = block_plan(send_peer, recv_from, own_group, group_count)
    flat_rows, key_flat, value_flat = attention_backward(
        hidden, queries, out_grad, counts.astype(jnp.float32), pair[:, :width], pair[:, width:]
    )
    pair_delta = jnp.concatenate([key_flat, value_flat], axis=1)
    slots, tokens = hidden.shape[0], hidden.shape[1]
    pair_rows = pair_delta.reshape(slots, tokens, 2 * width)
    leaving = select_rows(chosen, pair_rows)
    hidden_grad, pieces = reduce_back(recv_from, pair_delta, leaving, hidden, w_blocks)
    own_core = lax.rem(lax.axis_index("fsdp"), 2)
    rows = key_weight.shape[0]
    outer = pieces.reshape(2, width, 2 * rows)
    inner = jnp.swapaxes(pieces[..., 256:512], 1, 2).reshape(2, width, 256)
    grads = jnp.concatenate([outer[..., :256], inner, outer[..., 512:]], axis=-1)
    grads = lax.dynamic_slice_in_dim(grads, own_core * rows, rows, axis=2)
    grads = jnp.swapaxes(grads, 1, 2).astype(jnp.float32)
    return (hidden_grad, grads[0], grads[1])


def solution(mesh):
    return jax.shard_map(
        body,
        mesh=mesh,
        in_specs=(
            P(("dp", "fsdp"), None, None),
            P(("dp", "fsdp"), None, None),
            P(("dp", "fsdp"), None, None),
            P(("dp", "fsdp")),
            P(("dp", "fsdp")),
            P(("dp", "fsdp")),
            P("fsdp", None),
            P("fsdp", None),
        ),
        out_specs=(P(("dp", "fsdp"), None, None), P("fsdp", None), P("fsdp", None)),
        check_vma=False,
    )
```

```python
import jax
import jax.numpy as jnp
from jax import lax
from jax.experimental import pallas as pl
from jax.experimental.pallas import tpu as pltpu
from jax.sharding import PartitionSpec as P

HD = 128
JBLK = 16
WIDE = 384
MESH = pl.DeviceIdType.MESH


def place():
    d, f = lax.axis_index("dp"), lax.axis_index("fsdp")
    return lax.rem(lax.div(f, 2), 4), lax.div(f, 8), lax.rem(d, 2), lax.div(d, 2), lax.rem(f, 2)


def device(x, h, l, z, c):
    return (z * 2 + l, (h * 4 + x) * 2 + c)


def gather_kernel(hidden, kw, vw, pair_out, w_out, w, hid, send_sem, recv_sem, local_sem):
    x, h, l, z, c = place()
    rows, width = kw.shape
    cols = 2 * width
    quarter = rows // 4

    def wrap(v):
        return lax.rem(v + 4, 4)

    xp, xm = device(wrap(x + 1), h, l, z, c), device(wrap(x - 1), h, l, z, c)
    zp, zm = device(x, h, l, wrap(z + 1), c), device(x, h, l, wrap(z - 1), c)
    yo, peer = device(x, 1 - h, 1 - l, z, c), device(x, h, l, z, 1 - c)

    hid_copy = pltpu.make_async_copy(hidden, hid, local_sem.at[0])
    hid_copy.start()
    own = (h * 4 + x) * 2 + c
    w[own, :, pl.ds(0, width)] = kw[...]
    w[own, :, pl.ds(width, width)] = vw[...]

    barrier = pltpu.get_barrier_semaphore()
    for other in (xp, xm, zp, zm, yo, peer):
        pl.semaphore_signal(barrier, inc=1, device_id=other, device_id_type=MESH)
    pl.semaphore_wait(barrier, 6)

    number = {}
    started = []

    def copy(name, f, row, col, target):
        i = number.setdefault(name, len(number))
        ref = w.at[f, pl.ds(*row), pl.ds(*col)]
        return pltpu.make_async_remote_copy(
            src_ref=ref, dst_ref=ref, send_sem=send_sem.at[i], recv_sem=recv_sem.at[i],
            device_id=target, device_id_type=MESH,
        )

    def send(name, f, row, col, target):
        one = copy(name, f, row, col, target)
        one.start()
        started.append(one)

    def arrive(name, f, row, col):
        copy(name, f, row, col, peer).wait_recv()

    def block(hh, dx, core=c):
        return (hh * 4 + wrap(x + dx)) * 2 + core

    def part(dz):
        return (pl.multiple_of(wrap(z + dz) * quarter, quarter), quarter)

    def halves(odd):
        first = 256 if odd else 384
        return (WIDE, first), (WIDE + first, cols - WIDE - first)

    side = (h, 1 - h)
    narrow, wide = (WIDE, cols - WIDE), (0, WIDE)
    whole, low, high = (0, rows), (0, rows // 2), (rows // 2, rows // 2)

    send("cy", own, part(0), narrow, yo)
    send("cxp0", own, part(0), narrow, xp)
    send("cxm0", own, part(0), narrow, xm)
    send("own", own, whole, (0, cols), peer)

    def along_z(b, f):
        send(f"zp{b}", f, part(0), narrow, zp)
        send(f"zm{b}", f, part(0), narrow, zm)

    order = [(1, 0), (0, -1), (0, 1), (1, -1), (1, 1), (0, 2), (1, 2)]
    arrive("cy", block(side[1], 0), part(0), narrow)
    send("cxp1", block(side[1], 0), part(0), narrow, xp)
    send("cxm1", block(side[1], 0), part(0), narrow, xm)
    along_z(0, block(side[1], 0))
    for s in (0, 1):
        one, two = halves(s)
        arrive(f"cxp{s}", block(side[s], -1), part(0), narrow)
        send(f"cfp{s}", block(side[s], -1), part(0), one, xp)
        along_z(1 + 2 * s, block(side[s], -1))
        arrive(f"cxm{s}", block(side[s], 1), part(0), narrow)
        send(f"cfm{s}", block(side[s], 1), part(0), two, xm)
        along_z(2 + 2 * s, block(side[s], 1))
    send("ay", own, whole, wide, yo)
    send("axp0", own, whole, wide, xp)
    send("axm0", own, whole, wide, xm)
    for s in (0, 1):
        one, two = halves(s)
        arrive(f"cfp{s}", block(side[s], 2), part(0), one)
        arrive(f"cfm{s}", block(side[s], 2), part(0), two)
        along_z(5 + s, block(side[s], 2))

    def forward_z(b):
        s, dx = order[b]
        one, two = halves(b % 2)
        f = block(side[s], dx)
        arrive(f"zp{b}", f, part(-1), narrow)
        send(f"zfp{b}", f, part(-1), one, zp)
        arrive(f"zm{b}", f, part(1), narrow)
        send(f"zfm{b}", f, part(1), two, zm)

    def finish_z(b):
        s, dx = order[b]
        one, two = halves(b % 2)
        f = block(side[s], dx)
        arrive(f"zfp{b}", f, part(2), one)
        arrive(f"zfm{b}", f, part(2), two)
        send(f"pc{b}", f, whole, narrow, peer)

    def forward_x(s):
        arrive(f"axp{s}", block(side[s], -1), whole, wide)
        send(f"afp{s}", block(side[s], -1), low, wide, xp)
        arrive(f"axm{s}", block(side[s], 1), whole, wide)
        send(f"afm{s}", block(side[s], 1), high, wide, xm)
        send(f"pa{1 + 2 * s}", block(side[s], -1), whole, wide, peer)
        send(f"pa{2 + 2 * s}", block(side[s], 1), whole, wide, peer)

    forward_z(0)
    forward_z(1)
    arrive("ay", block(side[1], 0), whole, wide)
    send("axp1", block(side[1], 0), whole, wide, xp)
    send("axm1", block(side[1], 0), whole, wide, xm)
    send("pa0", block(side[1], 0), whole, wide, peer)
    forward_z(2)
    forward_z(3)
    forward_x(0)
    forward_z(4)
    forward_z(5)
    finish_z(0)
    finish_z(1)
    forward_z(6)
    forward_x(1)
    for b in range(2, 6):
        finish_z(b)
    for s in (0, 1):
        arrive(f"afp{s}", block(side[s], 2), low, wide)
        arrive(f"afm{s}", block(side[s], 2), high, wide)
        send(f"pa{5 + s}", block(side[s], 2), whole, wide, peer)
    finish_z(6)
    arrive("own", block(side[0], 0, 1 - c), whole, (0, cols))
    for b in range(7):
        s, dx = order[b]
        arrive(f"pa{b}", block(side[s], dx, 1 - c), whole, wide)
        arrive(f"pc{b}", block(side[s], dx, 1 - c), whole, narrow)
    w_copy = pltpu.make_async_copy(w, w_out, local_sem.at[1])
    w_copy.start()
    hid_copy.wait()

    blocks = w.shape[0]
    tokens = hidden.shape[0] * hidden.shape[1]
    group = 4

    @pl.loop(0, cols // 256)
    def _(n):
        at = pl.ds(pl.multiple_of(n * 256, 256), 256)
        total = jnp.zeros((tokens, 256), jnp.float32)
        for k in range(blocks // group):
            left = hid[:, :, pl.ds(k * group * rows, group * rows)].reshape(tokens, group * rows)
            right = w[pl.ds(k * group, group), :, at].reshape(group * rows, 256)
            total = total + jnp.dot(left, right, preferred_element_type=jnp.float32)
        pair_out[:, at] = total.astype(jnp.bfloat16)

    w_copy.wait()
    for one in started:
        one.wait_send()


def gather_project(hidden, key_weight, value_weight):
    rows, width = key_weight.shape
    tokens = hidden.shape[0] * hidden.shape[1]
    blocks = lax.axis_size("fsdp")
    vmem = pl.BlockSpec(memory_space=pltpu.VMEM)
    hbm = pl.BlockSpec(memory_space=pl.ANY)
    return pl.pallas_call(
        gather_kernel,
        name="gather_project",
        out_shape=(
            jax.ShapeDtypeStruct((tokens, 2 * width), jnp.bfloat16),
            jax.ShapeDtypeStruct((blocks, rows, 2 * width), jnp.bfloat16),
        ),
        in_specs=[hbm, vmem, vmem],
        out_specs=(vmem, hbm),
        scratch_shapes=[
            pltpu.VMEM((blocks, rows, 2 * width), jnp.bfloat16),
            pltpu.VMEM(hidden.shape, jnp.bfloat16),
            pltpu.SemaphoreType.DMA((64,)),
            pltpu.SemaphoreType.DMA((64,)),
            pltpu.SemaphoreType.DMA((2,)),
        ],
        compiler_params=pltpu.CompilerParams(
            collective_id=0, has_side_effects=True, vmem_limit_bytes=48 << 20
        ),
        cost_estimate=pl.CostEstimate(
            flops=2 * tokens * blocks * rows * 2 * width, bytes_accessed=22 << 20, transcendentals=0
        ),
    )(hidden, key_weight, value_weight)


def attend(counts, queries, grads, pair, delta, group):
    f32, bf16 = jnp.float32, jnp.bfloat16
    tokens = queries.shape[1]
    n = 4 * tokens
    half = pair.shape[1] // 2
    heads = half // HD
    share = queries.shape[2] // half
    scale = HD ** (-0.5)
    at = pl.ds(pl.multiple_of(group * n, n), n)
    slots = pl.ds(group * 4, 4)
    count = [counts[group * 4 + j].astype(f32) for j in range(4)]

    def per_slot(slot):
        return jnp.where(
            slot == 0, count[0], jnp.where(slot == 1, count[1], jnp.where(slot == 2, count[2], count[3]))
        )

    row = lax.broadcasted_iota(jnp.int32, (n, HD), 0)
    own = per_slot(lax.div(row, tokens))
    weight = jnp.where(lax.rem(row, tokens).astype(f32) < own * JBLK, 1.0, 0.0) / own
    lane = lax.broadcasted_iota(jnp.int32, (tokens, share * n), 1)
    slot = lax.div(lax.rem(lane, n), tokens)
    u = lax.broadcasted_iota(jnp.int32, (tokens, share * n), 0)
    allowed = (u <= lax.rem(lane, tokens)) & (u.astype(f32) < per_slot(slot) * JBLK)

    def fold(wide):
        a, b, c, d = (wide[j * tokens : (j + 1) * tokens] for j in range(4))
        return jnp.where(slot == 0, a, jnp.where(slot == 1, b, jnp.where(slot == 2, c, d)))

    def spread(narrow):
        parts = [jnp.where(slot == j, narrow, 0.0) for j in range(4)]
        return jnp.concatenate(parts, axis=0).astype(bf16)

    def across(a, b):
        return lax.dot_general(a, b, (((1,), (1,)), ((), ())), preferred_element_type=f32)

    for g in range(heads):
        cols = [slice((g * share + r) * HD, (g * share + r + 1) * HD) for r in range(share)]
        q = jnp.concatenate([queries[slots, :, c].reshape(n, HD) for c in cols], axis=0)
        od = jnp.concatenate(
            [(grads[slots, :, c].reshape(n, HD).astype(f32) * weight).astype(bf16) for c in cols],
            axis=0,
        )
        key = pair[at, g * HD : (g + 1) * HD]
        value = pair[at, half + g * HD : half + (g + 1) * HD]
        scores = jnp.where(allowed, fold(across(key, q)) * scale, -1e30)
        terms = jnp.exp(scores - jnp.max(scores, axis=0, keepdims=True))
        probs = terms / jnp.sum(terms, axis=0, keepdims=True)
        probs_half = probs.astype(bf16).astype(f32)
        prob_delta = fold(across(value, od))
        row_delta = jnp.sum(probs_half * prob_delta, axis=0, keepdims=True)
        score_delta = probs * (prob_delta - row_delta) * scale
        key_delta = jnp.dot(spread(score_delta), q, preferred_element_type=f32)
        value_delta = jnp.dot(spread(probs_half), od, preferred_element_type=f32)
        delta[at, g * HD : (g + 1) * HD] = key_delta.astype(bf16)
        delta[at, half + g * HD : half + (g + 1) * HD] = value_delta.astype(bf16)


def attend_kernel(counts, queries, grads, pair, delta):
    @pl.loop(0, queries.shape[0] // 4)
    def _(group):
        attend(counts, queries, grads, pair, delta, group)


def attend_all(counts, queries, grads, pair):
    vmem = pl.BlockSpec(memory_space=pltpu.VMEM)
    return pl.pallas_call(
        attend_kernel,
        name="attend",
        out_shape=jax.ShapeDtypeStruct(pair.shape, pair.dtype),
        in_specs=[pl.BlockSpec(memory_space=pltpu.SMEM), vmem, vmem, vmem],
        out_specs=vmem,
        compiler_params=pltpu.CompilerParams(vmem_limit_bytes=48 << 20),
    )(counts, queries, grads, pair)


def reduce_kernel(
    recv, pair, leaving, hidden, w_in, hg_out, gt_out,
    hid, w, dt, arrived, settled, hgb, summed, give, take,
    p0_half, p0_last, p1_half, p1_last, p2_half, p2_last,
    p0_two, p1_two, p2_two, p0_three, p1_three, p2_three, done,
    send_sem, recv_sem, local_sem,
):
    x, h, l, z, c = place()
    me = lax.axis_index("dp")
    y = 2 * h + l
    half = dt.shape[1]
    span = summed.shape[2]
    slots, tokens, _ = hidden.shape
    total = slots * tokens
    f32, bf16 = jnp.float32, jnp.bfloat16

    def wrap(v):
        return lax.rem(v + 4, 4)

    def at(dx=0, dy=0, dz=0, core=c):
        q = wrap(y + dy)
        return device(wrap(x + dx), lax.div(q, 2), lax.rem(q, 2), wrap(z + dz), core)

    xp, xm, x2 = at(dx=1), at(dx=-1), at(dx=2)
    yp, ym, y2 = at(dy=1), at(dy=-1), at(dy=2)
    zp, zm, z2 = at(dz=1), at(dz=-1), at(dz=2)
    peer = at(core=1 - c)
    twin = device(x, h, 1 - l, z, c)
    group = lax.axis_size("dp")
    f = lax.axis_index("fsdp")

    hid_copy = pltpu.make_async_copy(hidden, hid, local_sem.at[0])
    hid_copy.start()
    w_copy = pltpu.make_async_copy(w_in, w, local_sem.at[1])
    w_copy.start()

    others = [(lax.rem(me + j, group), f) for j in range(1, group)]
    others += [xp, xm, x2, device(x, 1 - h, 1 - l, z, c), y2, peer]
    barrier = pltpu.get_barrier_semaphore()
    for other in others:
        pl.semaphore_signal(barrier, inc=1, device_id=other, device_id_type=MESH)
    pl.semaphore_wait(barrier, len(others))

    number = {}
    started = []

    def copy(name, src, dst, target):
        i = number.setdefault(name, len(number))
        return pltpu.make_async_remote_copy(
            src_ref=src, dst_ref=dst, send_sem=send_sem.at[i], recv_sem=recv_sem.at[i],
            device_id=target, device_id_type=MESH,
        )

    def send(name, src, dst, target):
        one = copy(name, src, dst, target)
        one.start()
        started.append(one)

    def arrive(name, dst):
        copy(name, dst, dst, peer).wait_recv()

    def add(*refs):
        value = refs[0][...].astype(f32)
        for ref in refs[1:]:
            value = value + ref[...].astype(f32)
        return value.astype(bf16)

    arrived[me] = jnp.zeros(arrived.shape[1:], bf16)
    for j in range(1, group):
        to = lax.rem(me + j, group)
        send(f"a{j}", leaving.at[to], arrived.at[me], (to, f))
    for t in (0, 1):
        dt[t] = pair[:, t * half : (t + 1) * half].T

    lanes = (pl.ds(0, 256), pl.ds(256, 256), pl.ds(512, 128))
    order = [(0, 2), (1, 2), (1, 1), (0, -1), (0, 1), (1, -1), (0, 0), (1, 0)]

    def index(hh, dx):
        return hh * 4 + wrap(x + dx)

    def term(t, k):
        cols = pl.ds(pl.multiple_of(k * span, 128), span)
        return jnp.dot(dt[t], hid[:, :, cols].reshape(total, span), preferred_element_type=f32)

    def other_half(i):
        k = index(*order[i])
        give[k] = term(1 - c, k).astype(bf16)
        send(f"d{i}", give.at[k], take.at[k], peer)

    def own_half(i):
        k = index(*order[i])
        value = term(c, k)
        arrive(f"d{i}", take.at[k])
        summed[k] = (value + take[k].astype(f32)).astype(bf16)

    def zrows(dz):
        return pl.ds(pl.multiple_of(wrap(z + dz) * 128, 128), 128)

    def part1_first(i):
        k = index(*order[i])
        up, down = (2, -1) if i % 2 == 0 else (1, 2)
        one, two = ("h", "n") if i % 2 == 0 else ("n", "h")
        far_dst, near_dst = p1_half.at[i], p1_last.at[1 if i % 2 == 0 else 0, i]
        dst = {"h": far_dst, "n": near_dst}
        send(f"z{one}{i}", summed.at[k, zrows(up), lanes[1]], dst[one], zp)
        send(f"z{two}{i}", summed.at[k, zrows(down), lanes[1]], dst[two], zm)

    def part1_second(i):
        k = index(*order[i])
        near, target = (1, zp) if i % 2 == 0 else (-1, zm)
        arrive(f"zh{i}", p1_half.at[i])
        ref = summed.at[k, zrows(near), lanes[1]]
        ref[...] = add(ref, p1_half.at[i])
        send(f"zl{i}", ref, p1_last.at[0 if i % 2 == 0 else 1, i], target)

    def part1_last(i):
        k = index(*order[i])
        arrive(f"zn{i}", p1_last.at[1 if i % 2 == 0 else 0, i])
        arrive(f"zl{i}", p1_last.at[0 if i % 2 == 0 else 1, i])
        ref = summed.at[k, zrows(0), lanes[1]]
        ref[...] = add(ref, p1_last.at[0, i], p1_last.at[1, i])

    def yref(dy, dx):
        q = wrap(y + dy)
        rows = pl.ds(pl.multiple_of(lax.rem(q, 2) * 256, 256), 256)
        return summed.at[lax.div(q, 2) * 4 + wrap(x + dx), rows, lanes[2]]

    shifts = (2, 1, -1, 0)

    def part2_first(j):
        dx = shifts[j]
        if j % 2 == 0:
            send(f"yh{j}", yref(2, dx), p2_half.at[j], yp)
            send(f"yn{j}", yref(-1, dx), p2_last.at[1, j], ym)
        else:
            send(f"yn{j}", yref(1, dx), p2_last.at[0, j], yp)
            send(f"yh{j}", yref(2, dx), p2_half.at[j], ym)

    def part2_second(j):
        near, target = (1, yp) if j % 2 == 0 else (-1, ym)
        arrive(f"yh{j}", p2_half.at[j])
        ref = yref(near, shifts[j])
        ref[...] = add(ref, p2_half.at[j])
        send(f"yl{j}", ref, p2_last.at[0 if j % 2 == 0 else 1, j], target)

    def part2_last(j):
        arrive(f"yn{j}", p2_last.at[1 if j % 2 == 0 else 0, j])
        arrive(f"yl{j}", p2_last.at[0 if j % 2 == 0 else 1, j])
        ref = yref(0, shifts[j])
        ref[...] = add(ref, p2_last.at[0, j], p2_last.at[1, j])

    def xref(hh, dx):
        return summed.at[index(hh, dx), :, lanes[0]]

    hid_copy.wait()
    other_half(0)
    other_half(1)
    for i in range(8):
        own_half(i)
        if i == 0:
            send("xh0", xref(0, 2), p0_half.at[0], xp)
        elif i == 1:
            send("xh1", xref(1, 2), p0_half.at[1], xm)
        elif i == 2:
            send("xn1", xref(1, 1), p0_last.at[0, 1], xp)
        elif i == 3:
            send("xn0", xref(0, -1), p0_last.at[1, 0], xm)
        part1_first(i)
        if i == 1:
            part2_first(0)
        elif i == 5:
            part2_first(1)
            part2_first(2)
        elif i == 7:
            part2_first(3)
        if i + 2 < 8:
            other_half(i + 2)
        if i >= 3:
            part1_second(i - 3)
        if i == 5:
            part2_second(0)
    arrive("xh0", p0_half.at[0])
    xref(0, 1)[...] = add(xref(0, 1), p0_half.at[0])
    send("xl0", xref(0, 1), p0_last.at[0, 0], xp)
    arrive("xh1", p0_half.at[1])
    xref(1, -1)[...] = add(xref(1, -1), p0_half.at[1])
    send("xl1", xref(1, -1), p0_last.at[1, 1], xm)
    part1_second(5)
    part2_second(1)
    part2_second(2)

    for j in range(1, group):
        arrive(f"a{j}", arrived.at[lax.rem(me + group - j, group)])
    for s in range(slots):
        source = recv[s]
        kept = pair[pl.ds(s * tokens, tokens), :]
        settled[pl.ds(s * tokens, tokens), :] = jnp.where(source == me, kept, arrived[source])
    w_copy.wait()
    hg_copies = []

    def back(j):
        block = w[2 * j : 2 * j + 2].reshape(span, w.shape[2])
        value = lax.dot_general(
            settled[...], block, (((1,), (1,)), ((), ())), preferred_element_type=f32
        )
        cols = pl.ds(j * span, span)
        hgb[:, :, cols] = value.astype(bf16).reshape(slots, tokens, span)
        one = pltpu.make_async_copy(hgb.at[:, :, cols], hg_out.at[:, :, cols], local_sem.at[2 + j])
        one.start()
        hg_copies.append(one)

    back(0)
    part1_second(6)
    back(1)
    part2_second(3)
    part1_second(7)
    for i in range(4):
        part1_last(i)
    back(2)
    part2_last(0)
    part1_last(4)
    part1_last(5)
    back(3)
    part2_last(1)
    part2_last(2)
    back(4)
    part2_last(3)
    part1_last(6)
    part1_last(7)

    steps = ((1, xp), (-1, xm), (2, x2))
    for n, (dx, target) in enumerate(steps):
        for hh in (0, 1):
            src = summed.at[index(hh, dx), zrows(0), lanes[1]]
            send(f"s1{n}{hh}", src, p1_two.at[n, hh], target)

    def zpiece(dz):
        rows = pl.ds(pl.multiple_of(l * 256 + wrap(z + dz) * 64, 64), 64)
        return summed.at[pl.ds(pl.multiple_of(h * 4, 4), 4), rows, lanes[2]]

    for n, (dz, target) in enumerate(((1, zp), (-1, zm), (2, z2))):
        send(f"s2{n}", zpiece(dz), p2_two.at[n], target)
    for hh in (0, 1):
        arrive(f"xn{hh}", p0_last.at[1 - hh, hh])
        arrive(f"xl{hh}", p0_last.at[hh, hh])
        xref(hh, 0)[...] = add(xref(hh, 0), p0_last.at[0, hh], p0_last.at[1, hh])

    def ypiece(dy):
        q = wrap(y + dy)
        rows = pl.ds(pl.multiple_of(lax.rem(q, 2) * 256, 256), 256)
        return summed.at[lax.div(q, 2) * 4 + x, rows, lanes[0]]

    for n, (dy, target) in enumerate(((1, yp), (-1, ym), (2, y2))):
        send(f"s0{n}", ypiece(dy), p0_two.at[n], target)
    back(5)
    for n in range(3):
        arrive(f"s2{n}", p2_two.at[n])
    zpiece(0)[...] = add(zpiece(0), p2_two.at[0], p2_two.at[1], p2_two.at[2])

    piece_rows = pl.ds(pl.multiple_of(l * 256 + z * 64, 64), 64)
    for n, (dx, target) in enumerate(steps):
        send(f"t2{n}", summed.at[index(h, dx), piece_rows, lanes[2]], p2_three.at[n], target)
    back(6)
    for n in range(3):
        for hh in (0, 1):
            arrive(f"s1{n}{hh}", p1_two.at[n, hh])
    for hh in (0, 1):
        ref = summed.at[index(hh, 0), zrows(0), lanes[1]]
        ref[...] = add(ref, p1_two.at[0, hh], p1_two.at[1, hh], p1_two.at[2, hh])

    def third1(dy):
        q = wrap(y + dy)
        rows = pl.ds(pl.multiple_of(z * 128 + lax.rem(q, 2) * 64, 64), 64)
        return summed.at[lax.div(q, 2) * 4 + x, rows, lanes[1]]

    for n, (dy, target) in enumerate(((1, yp), (-1, ym), (2, y2))):
        send(f"t1{n}", third1(dy), p1_three.at[n], target)
    back(7)
    for n in range(3):
        arrive(f"s0{n}", p0_two.at[n])
    ypiece(0)[...] = add(ypiece(0), p0_two.at[0], p0_two.at[1], p0_two.at[2])

    def third0(dz):
        rows = pl.ds(pl.multiple_of(l * 256 + wrap(z + dz) * 64, 64), 64)
        return summed.at[h * 4 + x, rows, lanes[0]]

    for n, (dz, target) in enumerate(((1, zp), (-1, zm), (2, z2))):
        send(f"t0{n}", third0(dz), p0_three.at[n], target)

    def finish(part, ref, buffer):
        for n in range(3):
            arrive(f"t{part}{n}", buffer.at[n])
        value = add(ref, buffer.at[0], buffer.at[1], buffer.at[2])
        mine = done.at[c, l, z, :, lanes[part]]
        mine[...] = value
        send(f"gy{part}", mine, mine, twin)
        send(f"gp{part}", mine, mine, zp)
        send(f"gm{part}", mine, mine, zm)
        send(f"g2{part}", mine, mine, z2)

    def pass_on(part):
        def piece(ll, dz):
            return done.at[c, ll, wrap(z + dz), :, lanes[part]]

        arrive(f"gy{part}", piece(1 - l, 0))
        send(f"fp{part}", piece(1 - l, 0), piece(1 - l, 0), zp)
        send(f"fm{part}", piece(1 - l, 0), piece(1 - l, 0), zm)
        arrive(f"g2{part}", piece(l, 2))
        send(f"fy{part}", piece(l, 2), piece(l, 2), twin)

    def collect(part):
        def piece(ll, dz):
            return done.at[c, ll, wrap(z + dz), :, lanes[part]]

        arrive(f"gp{part}", piece(l, -1))
        arrive(f"gm{part}", piece(l, 1))
        arrive(f"fp{part}", piece(1 - l, -1))
        arrive(f"fm{part}", piece(1 - l, 1))
        arrive(f"fy{part}", piece(1 - l, 2))
        ref = done.at[c, :, :, :, lanes[part]]
        send(f"e{part}", ref, ref, peer)

    finish(2, summed.at[h * 4 + x, piece_rows, lanes[2]], p2_three)
    finish(1, third1(0), p1_three)
    pass_on(2)
    finish(0, third0(0), p0_three)
    pass_on(1)
    collect(2)
    pass_on(0)
    collect(1)
    collect(0)
    for part in (2, 1, 0):
        arrive(f"e{part}", done.at[1 - c, :, :, :, lanes[part]])
    out_copy = pltpu.make_async_copy(done, gt_out, local_sem.at[10])
    out_copy.start()
    for one in started:
        one.wait_send()
    for one in hg_copies:
        one.wait()
    out_copy.wait()


def reduce_back(recv_from, pair, leaving, hidden, w_blocks):
    blocks, rows, cols = w_blocks.shape
    half, span = cols // 2, 2 * rows
    chips = blocks // 2
    total = pair.shape[0]
    bf16 = jnp.bfloat16
    vmem = pl.BlockSpec(memory_space=pltpu.VMEM)
    hbm = pl.BlockSpec(memory_space=pl.ANY)
    buffer = lambda *shape: pltpu.VMEM(shape, bf16)
    return pl.pallas_call(
        reduce_kernel,
        name="reduce_back",
        out_shape=(
            jax.ShapeDtypeStruct(hidden.shape, bf16),
            jax.ShapeDtypeStruct((2, 2, 4, half // 8, span), bf16),
        ),
        in_specs=[pl.BlockSpec(memory_space=pltpu.SMEM), vmem, vmem, hbm, hbm],
        out_specs=(hbm, hbm),
        scratch_shapes=[
            buffer(*hidden.shape),
            buffer(blocks, rows, cols),
            buffer(2, half, total),
            buffer(*leaving.shape),
            buffer(total, cols),
            buffer(*hidden.shape),
            buffer(chips, half, span),
            buffer(chips, half, span),
            buffer(chips, half, span),
            buffer(2, half, 256),
            buffer(2, 2, half, 256),
            buffer(8, half // 4, 256),
            buffer(2, 8, half // 4, 256),
            buffer(4, half // 2, 128),
            buffer(2, 4, half // 2, 128),
            buffer(3, half // 2, 256),
            buffer(3, 2, half // 4, 256),
            buffer(3, 4, half // 8, 128),
            buffer(3, half // 8, 256),
            buffer(3, half // 8, 256),
            buffer(3, half // 8, 128),
            buffer(2, 2, 4, half // 8, span),
            pltpu.SemaphoreType.DMA((112,)),
            pltpu.SemaphoreType.DMA((112,)),
            pltpu.SemaphoreType.DMA((11,)),
        ],
        compiler_params=pltpu.CompilerParams(
            collective_id=1, has_side_effects=True, vmem_limit_bytes=60 << 20
        ),
        cost_estimate=pl.CostEstimate(
            flops=4 * total * blocks * rows * cols, bytes_accessed=22 << 20, transcendentals=0
        ),
    )(recv_from, pair, leaving, hidden, w_blocks)


def finish_kernel(hg_in, pieces_in, hg_out, key_grad, value_grad, hg, pieces, sem):
    chunks = 8
    step = hg.shape[0] // chunks
    first = pltpu.make_async_copy(pieces_in, pieces, sem.at[2 * chunks])
    first.start()

    def chunk(i, src, dst, offset):
        at = pl.ds(i * step, step)
        return pltpu.make_async_copy(src.at[at], dst.at[at], sem.at[offset + i])

    for i in range(chunks):
        chunk(i, hg_in, hg, 0).start()
    first.wait()
    for i in range(chunks):
        chunk(i, hg_in, hg, 0).wait()
        chunk(i, hg, hg_out, chunks).start()
    core = lax.rem(lax.axis_index("fsdp"), 2)
    rows, width = key_grad.shape
    for t, out in enumerate((key_grad, value_grad)):
        outer = pieces[t].reshape(width, 2 * rows)
        inner = jnp.concatenate(
            [pieces[t, l, z, :, 256:512] for z in range(4) for l in range(2)], axis=0
        )
        grads = jnp.concatenate([outer[:, :256], inner, outer[:, 512:]], axis=1)
        grads = grads.astype(jnp.float32)
        out[...] = jnp.where(core == 0, grads[:, :rows], grads[:, rows:]).T
    for i in range(chunks):
        chunk(i, hg, hg_out, chunks).wait()


def finish(hidden_grad, pieces):
    rows, width = pieces.shape[-1] // 2, pieces.shape[1] * pieces.shape[2] * pieces.shape[3]
    vmem = pl.BlockSpec(memory_space=pltpu.VMEM)
    hbm = pl.BlockSpec(memory_space=pl.ANY)
    grad = jax.ShapeDtypeStruct((rows, width), jnp.float32)
    return pl.pallas_call(
        finish_kernel,
        name="finish",
        out_shape=(jax.ShapeDtypeStruct(hidden_grad.shape, hidden_grad.dtype), grad, grad),
        in_specs=[hbm, hbm],
        out_specs=(hbm, vmem, vmem),
        scratch_shapes=[
            pltpu.VMEM(hidden_grad.shape, hidden_grad.dtype),
            pltpu.VMEM(pieces.shape, pieces.dtype),
            pltpu.SemaphoreType.DMA((17,)),
        ],
        compiler_params=pltpu.CompilerParams(vmem_limit_bytes=60 << 20),
    )(hidden_grad, pieces)


def block_plan(send_peer, recv_from, own_group, group_count):
    peer_ids = jnp.arange(group_count, dtype=jnp.int32)
    staying = recv_from == own_group
    chosen = ((send_peer[None, :] == peer_ids[:, None]) & (peer_ids[:, None] != own_group)).astype(
        jnp.bfloat16
    )
    placing = (
        (recv_from[:, None] == peer_ids[None, :]) & jnp.logical_not(staying)[:, None]
    ).astype(jnp.bfloat16)
    return (chosen, placing, staying)


def select_rows(chosen, source):
    return jnp.einsum("ps,stf->ptf", chosen, source, preferred_element_type=jnp.float32).astype(
        jnp.bfloat16
    )


def body(hidden, queries, out_grad, counts, send_peer, recv_from, key_weight, value_weight):
    width = key_weight.shape[1]
    pair, w_blocks = gather_project(hidden, key_weight, value_weight)
    group_count = lax.axis_size("dp")
    own_group = lax.axis_index("dp")
    chosen, placing, staying = block_plan(send_peer, recv_from, own_group, group_count)
    pair_delta = attend_all(counts, queries, out_grad, pair)
    slots, tokens = hidden.shape[0], hidden.shape[1]
    pair_rows = pair_delta.reshape(slots, tokens, 2 * width)
    leaving = select_rows(chosen, pair_rows)
    hidden_grad, pieces = reduce_back(recv_from, pair_delta, leaving, hidden, w_blocks)
    return finish(hidden_grad, pieces)


def solution(mesh):
    return jax.shard_map(
        body,
        mesh=mesh,
        in_specs=(
            P(("dp", "fsdp"), None, None),
            P(("dp", "fsdp"), None, None),
            P(("dp", "fsdp"), None, None),
            P(("dp", "fsdp")),
            P(("dp", "fsdp")),
            P(("dp", "fsdp")),
            P("fsdp", None),
            P("fsdp", None),
        ),
        out_specs=(P(("dp", "fsdp"), None, None), P("fsdp", None), P("fsdp", None)),
        check_vma=False,
    )
```

```python
import jax
import jax.numpy as jnp
from jax import lax
from jax.experimental import pallas as pl
from jax.experimental.pallas import tpu as pltpu
from jax.sharding import PartitionSpec as P

HD = 128
JBLK = 16
WIDE = 384
MESH = pl.DeviceIdType.MESH


def place():
    d, f = lax.axis_index("dp"), lax.axis_index("fsdp")
    return lax.rem(lax.div(f, 2), 4), lax.div(f, 8), lax.rem(d, 2), lax.div(d, 2), lax.rem(f, 2)


def device(x, h, l, z, c):
    return (z * 2 + l, (h * 4 + x) * 2 + c)


def attend(counts, queries, grads, pair, delta, group):
    f32, bf16 = jnp.float32, jnp.bfloat16
    tokens = queries.shape[1]
    n = 4 * tokens
    half = pair.shape[1] // 2
    heads = half // HD
    share = queries.shape[2] // half
    scale = HD ** (-0.5)
    at = pl.ds(pl.multiple_of(group * n, n), n)
    slots = pl.ds(group * 4, 4)
    count = [counts[group * 4 + j].astype(f32) for j in range(4)]

    def per_slot(slot):
        return jnp.where(
            slot == 0, count[0], jnp.where(slot == 1, count[1], jnp.where(slot == 2, count[2], count[3]))
        )

    row = lax.broadcasted_iota(jnp.int32, (n, HD), 0)
    own = per_slot(lax.div(row, tokens))
    weight = jnp.where(lax.rem(row, tokens).astype(f32) < own * JBLK, 1.0, 0.0) / own
    lane = lax.broadcasted_iota(jnp.int32, (tokens, share * n), 1)
    slot = lax.div(lax.rem(lane, n), tokens)
    u = lax.broadcasted_iota(jnp.int32, (tokens, share * n), 0)
    allowed = (u <= lax.rem(lane, tokens)) & (u.astype(f32) < per_slot(slot) * JBLK)

    def fold(wide):
        a, b, c, d = (wide[j * tokens : (j + 1) * tokens] for j in range(4))
        return jnp.where(slot == 0, a, jnp.where(slot == 1, b, jnp.where(slot == 2, c, d)))

    def spread(narrow):
        parts = [jnp.where(slot == j, narrow, 0.0) for j in range(4)]
        return jnp.concatenate(parts, axis=0).astype(bf16)

    def across(a, b):
        return lax.dot_general(a, b, (((1,), (1,)), ((), ())), preferred_element_type=f32)

    for g in range(heads):
        cols = [slice((g * share + r) * HD, (g * share + r + 1) * HD) for r in range(share)]
        q = jnp.concatenate([queries[slots, :, c].reshape(n, HD) for c in cols], axis=0)
        od = jnp.concatenate(
            [(grads[slots, :, c].reshape(n, HD).astype(f32) * weight).astype(bf16) for c in cols],
            axis=0,
        )
        key = pair[at, g * HD : (g + 1) * HD]
        value = pair[at, half + g * HD : half + (g + 1) * HD]
        scores = jnp.where(allowed, fold(across(key, q)) * scale, -1e30)
        terms = jnp.exp(scores - jnp.max(scores, axis=0, keepdims=True))
        probs = terms / jnp.sum(terms, axis=0, keepdims=True)
        probs_half = probs.astype(bf16).astype(f32)
        prob_delta = fold(across(value, od))
        row_delta = jnp.sum(probs_half * prob_delta, axis=0, keepdims=True)
        score_delta = probs * (prob_delta - row_delta) * scale
        key_delta = jnp.dot(spread(score_delta), q, preferred_element_type=f32)
        value_delta = jnp.dot(spread(probs_half), od, preferred_element_type=f32)
        delta[at, g * HD : (g + 1) * HD] = key_delta.astype(bf16)
        delta[at, half + g * HD : half + (g + 1) * HD] = value_delta.astype(bf16)


def main_kernel(
    counts, send_peer, recv_from, kw, vw, hidden, queries, out_grad, hg_out, gt_out,
    w, hid, qs, gs, acc, pair, delta, leaving, arrived, settled, dt, summed, give, take,
    p0_half, p0_last, p1_half, p1_last, p2_half, p2_last,
    p0_two, p1_two, p2_two, p0_three, p1_three, p2_three, done,
    send_sem, recv_sem, local_sem,
):
    x, h, l, z, c = place()
    me, f = lax.axis_index("dp"), lax.axis_index("fsdp")
    group = lax.axis_size("dp")
    y = 2 * h + l
    rows, width = kw.shape
    cols = 2 * width
    quarter = rows // 4
    half = width
    span = 2 * rows
    slots, tokens, _ = hidden.shape
    total = slots * tokens
    f32, bf16 = jnp.float32, jnp.bfloat16

    def wrap(v):
        return lax.rem(v + 4, 4)

    def at(dx=0, dy=0, dz=0, core=c):
        q = wrap(y + dy)
        return device(wrap(x + dx), lax.div(q, 2), lax.rem(q, 2), wrap(z + dz), core)

    xp, xm, x2 = at(dx=1), at(dx=-1), at(dx=2)
    yp, ym, y2 = at(dy=1), at(dy=-1), at(dy=2)
    zp, zm, z2 = at(dz=1), at(dz=-1), at(dz=2)
    peer = at(core=1 - c)
    twin, yo = device(x, h, 1 - l, z, c), device(x, 1 - h, 1 - l, z, c)

    loads = []
    for i, (src, dst) in enumerate(((hidden, hid), (queries, qs), (out_grad, gs))):
        loads.append(pltpu.make_async_copy(src, dst, local_sem.at[i]))
        loads[-1].start()
    hid_copy = loads[0]
    own = (h * 4 + x) * 2 + c
    w[own, :, pl.ds(0, width)] = kw[...]
    w[own, :, pl.ds(width, width)] = vw[...]

    others = [(lax.rem(me + j, group), f) for j in range(1, group)]
    others += [xp, xm, x2, yo, y2, peer]
    barrier = pltpu.get_barrier_semaphore()
    for other in others:
        pl.semaphore_signal(barrier, inc=1, device_id=other, device_id_type=MESH)
    pl.semaphore_wait(barrier, len(others))

    number = {}
    started = []

    def copy(name, src, dst, target):
        i = number.setdefault(name, len(number))
        return pltpu.make_async_remote_copy(
            src_ref=src, dst_ref=dst, send_sem=send_sem.at[i], recv_sem=recv_sem.at[i],
            device_id=target, device_id_type=MESH,
        )

    def send(name, src, dst, target):
        one = copy(name, src, dst, target)
        one.start()
        started.append(one)

    def arrive(name, dst):
        copy(name, dst, dst, peer).wait_recv()

    def w_send(name, block, row, col, target):
        ref = w.at[block, pl.ds(*row), pl.ds(*col)]
        send(name, ref, ref, target)

    def w_arrive(name, block, row, col):
        arrive(name, w.at[block, pl.ds(*row), pl.ds(*col)])

    def block(hh, dx, core=c):
        return (hh * 4 + wrap(x + dx)) * 2 + core

    def part(dz):
        return (pl.multiple_of(wrap(z + dz) * quarter, quarter), quarter)

    def halves(odd):
        first = 256 if odd else 384
        return (WIDE, first), (WIDE + first, cols - WIDE - first)

    side = (h, 1 - h)
    narrow, wide = (WIDE, cols - WIDE), (0, WIDE)
    whole, low, high = (0, rows), (0, rows // 2), (rows // 2, rows // 2)

    w_send("cy", own, part(0), narrow, yo)
    w_send("cxp0", own, part(0), narrow, xp)
    w_send("cxm0", own, part(0), narrow, xm)
    w_send("own", own, whole, (0, cols), peer)

    def along_z(b, f):
        w_send(f"zp{b}", f, part(0), narrow, zp)
        w_send(f"zm{b}", f, part(0), narrow, zm)

    blocks_in = [(1, 0), (0, -1), (0, 1), (1, -1), (1, 1), (0, 2), (1, 2)]

    def source(b):
        return block(side[blocks_in[b][0]], blocks_in[b][1])

    w_arrive("cy", source(0), part(0), narrow)
    w_send("cxp1", source(0), part(0), narrow, xp)
    w_send("cxm1", source(0), part(0), narrow, xm)
    along_z(0, source(0))
    for s in (0, 1):
        one, two = halves(s)
        w_arrive(f"cxp{s}", block(side[s], -1), part(0), narrow)
        w_send(f"cfp{s}", block(side[s], -1), part(0), one, xp)
        w_arrive(f"cxm{s}", block(side[s], 1), part(0), narrow)
        w_send(f"cfm{s}", block(side[s], 1), part(0), two, xm)
        if s == 0:
            along_z(1, source(1))
            along_z(2, source(2))
    w_send("ay", own, whole, wide, yo)
    w_send("axp0", own, whole, wide, xp)
    w_send("axm0", own, whole, wide, xm)
    for s in (0, 1):
        one, two = halves(s)
        w_arrive(f"cfp{s}", source(5 + s), part(0), one)
        w_arrive(f"cfm{s}", source(5 + s), part(0), two)

    def forward_z(b):
        s, dx = blocks_in[b]
        one, two = halves(b % 2)
        f = block(side[s], dx)
        w_arrive(f"zp{b}", f, part(-1), narrow)
        w_send(f"zfp{b}", f, part(-1), one, zp)
        w_arrive(f"zm{b}", f, part(1), narrow)
        w_send(f"zfm{b}", f, part(1), two, zm)

    def finish_z(b):
        s, dx = blocks_in[b]
        one, two = halves(b % 2)
        f = block(side[s], dx)
        w_arrive(f"zfp{b}", f, part(2), one)
        w_arrive(f"zfm{b}", f, part(2), two)
        w_send(f"pc{b}", f, whole, narrow, peer)

    def forward_x(s):
        w_arrive(f"axp{s}", block(side[s], -1), whole, wide)
        w_send(f"afp{s}", block(side[s], -1), low, wide, xp)
        w_arrive(f"axm{s}", block(side[s], 1), whole, wide)
        w_send(f"afm{s}", block(side[s], 1), high, wide, xm)
        w_send(f"pa{1 + 2 * s}", block(side[s], -1), whole, wide, peer)
        w_send(f"pa{2 + 2 * s}", block(side[s], 1), whole, wide, peer)

    def finish_x(s):
        w_arrive(f"afp{s}", source(5 + s), low, wide)
        w_arrive(f"afm{s}", source(5 + s), high, wide)
        w_send(f"pa{5 + s}", source(5 + s), whole, wide, peer)

    def project(b):
        if b < 0:
            w_arrive("own", block(h, 0, 1 - c), whole, (0, cols))
            k = h * 4 + x
        else:
            s, dx = blocks_in[b]
            w_arrive(f"pa{b}", block(side[s], dx, 1 - c), whole, wide)
            w_arrive(f"pc{b}", block(side[s], dx, 1 - c), whole, narrow)
            k = side[s] * 4 + wrap(x + dx)
        span = 2 * rows
        left = pl.ds(pl.multiple_of(k * span, 128), span)
        right = pl.ds(pl.multiple_of(k * 2, 2), 2)

        @pl.loop(0, cols // 256)
        def _(n):
            at = pl.ds(pl.multiple_of(n * 256, 256), 256)
            value = jnp.dot(
                hid[:, :, left].reshape(total, span),
                w[right, :, at].reshape(span, 256),
                preferred_element_type=jnp.float32,
            )
            if b < 0:
                acc[:, at] = value
            elif b < 6:
                acc[:, at] += value
            else:
                pair[:, at] = (acc[:, at] + value).astype(jnp.bfloat16)

    forward_z(0)
    along_z(3, source(3))
    forward_z(1)
    along_z(4, source(4))
    w_arrive("ay", source(0), whole, wide)
    w_send("axp1", source(0), whole, wide, xp)
    w_send("axm1", source(0), whole, wide, xm)
    w_send("pa0", source(0), whole, wide, peer)
    hid_copy.wait()
    project(-1)
    forward_z(2)
    along_z(5, source(5))
    forward_z(3)
    along_z(6, source(6))
    forward_x(0)
    finish_z(0)
    forward_z(4)
    finish_z(1)
    project(0)
    forward_z(5)
    forward_x(1)
    finish_z(2)
    project(1)
    forward_z(6)
    finish_z(3)
    project(2)
    finish_z(4)
    project(3)
    finish_x(0)
    finish_z(5)
    project(4)
    finish_x(1)
    finish_z(6)
    project(5)
    project(6)

    loads[1].wait()
    loads[2].wait()

    @pl.loop(0, slots // 4)
    def _(four):
        attend(counts, qs, gs, pair, delta, four)

    def add(*refs):
        value = refs[0][...].astype(f32)
        for ref in refs[1:]:
            value = value + ref[...].astype(f32)
        return value.astype(bf16)

    arrived[me] = jnp.zeros(arrived.shape[1:], bf16)
    for j in range(1, group):
        to = lax.rem(me + j, group)
        chosen = delta[pl.ds(0, tokens), :]
        for s in range(1, slots):
            here = delta[pl.ds(s * tokens, tokens), :]
            chosen = jnp.where(send_peer[s] == to, here, chosen)
        leaving[to] = chosen
        send(f"a{j}", leaving.at[to], arrived.at[me], (to, f))
    for t in (0, 1):
        dt[t] = delta[:, t * half : (t + 1) * half].T

    lanes = (pl.ds(0, 256), pl.ds(256, 384), pl.ds(256, 384))
    rest = (pl.ds(0, 64), pl.ds(0, 32), pl.ds(32, 32))
    order = [(0, 2), (1, 2), (1, 1), (0, -1), (0, 1), (1, -1), (0, 0), (1, 0)]

    def index(hh, dx):
        return hh * 4 + wrap(x + dx)

    def term(t, k):
        cut = pl.ds(pl.multiple_of(k * span, 128), span)
        return jnp.dot(dt[t], hid[:, :, cut].reshape(total, span), preferred_element_type=f32)

    def other_half(i):
        k = index(*order[i])
        give[k] = term(1 - c, k).astype(bf16).reshape(give.shape[1:])
        send(f"d{i}", give.at[k], take.at[k], peer)

    def own_half(i):
        k = index(*order[i])
        value = term(c, k)
        arrive(f"d{i}", take.at[k])
        summed[k] = (value + take[k].reshape(value.shape).astype(f32)).astype(bf16)

    def zrows(dz):
        return pl.ds(pl.multiple_of(wrap(z + dz) * 64, 64), 64)

    def part1_first(i):
        k = index(*order[i])
        up, down = (2, -1) if i % 2 == 0 else (1, 2)
        one, two = ("h", "n") if i % 2 == 0 else ("n", "h")
        far_dst, near_dst = p1_half.at[i], p1_last.at[1 if i % 2 == 0 else 0, i]
        dst = {"h": far_dst, "n": near_dst}
        send(f"z{one}{i}", summed.at[k, zrows(up), lanes[1]], dst[one], zp)
        send(f"z{two}{i}", summed.at[k, zrows(down), lanes[1]], dst[two], zm)

    def part1_second(i):
        k = index(*order[i])
        near, target = (1, zp) if i % 2 == 0 else (-1, zm)
        arrive(f"zh{i}", p1_half.at[i])
        ref = summed.at[k, zrows(near), lanes[1]]
        ref[...] = add(ref, p1_half.at[i])
        send(f"zl{i}", ref, p1_last.at[0 if i % 2 == 0 else 1, i], target)

    def part1_last(i):
        k = index(*order[i])
        arrive(f"zn{i}", p1_last.at[1 if i % 2 == 0 else 0, i])
        arrive(f"zl{i}", p1_last.at[0 if i % 2 == 0 else 1, i])
        ref = summed.at[k, zrows(0), lanes[1]]
        ref[...] = add(ref, p1_last.at[0, i], p1_last.at[1, i])

    def yref(dy, dx):
        q = wrap(y + dy)
        lower = pl.ds(pl.multiple_of(256 + lax.rem(q, 2) * 128, 128), 128)
        return summed.at[lax.div(q, 2) * 4 + wrap(x + dx), lower, lanes[2]]

    shifts = (2, 1, -1, 0)

    def part2_first(j):
        dx = shifts[j]
        if j % 2 == 0:
            send(f"yh{j}", yref(2, dx), p2_half.at[j], yp)
            send(f"yn{j}", yref(-1, dx), p2_last.at[1, j], ym)
        else:
            send(f"yn{j}", yref(1, dx), p2_last.at[0, j], yp)
            send(f"yh{j}", yref(2, dx), p2_half.at[j], ym)

    def part2_second(j):
        near, target = (1, yp) if j % 2 == 0 else (-1, ym)
        arrive(f"yh{j}", p2_half.at[j])
        ref = yref(near, shifts[j])
        ref[...] = add(ref, p2_half.at[j])
        send(f"yl{j}", ref, p2_last.at[0 if j % 2 == 0 else 1, j], target)

    def part2_last(j):
        arrive(f"yn{j}", p2_last.at[1 if j % 2 == 0 else 0, j])
        arrive(f"yl{j}", p2_last.at[0 if j % 2 == 0 else 1, j])
        ref = yref(0, shifts[j])
        ref[...] = add(ref, p2_last.at[0, j], p2_last.at[1, j])

    def xref(hh, dx):
        return summed.at[index(hh, dx), :, lanes[0]]

    other_half(0)
    other_half(1)
    for i in range(8):
        own_half(i)
        if i == 0:
            send("xh0", xref(0, 2), p0_half.at[0], xp)
        elif i == 1:
            send("xh1", xref(1, 2), p0_half.at[1], xm)
        elif i == 2:
            send("xn1", xref(1, 1), p0_last.at[0, 1], xp)
        elif i == 3:
            send("xn0", xref(0, -1), p0_last.at[1, 0], xm)
        part1_first(i)
        if i == 1:
            part2_first(0)
        elif i == 5:
            part2_first(1)
            part2_first(2)
        elif i == 7:
            part2_first(3)
        if i + 2 < 8:
            other_half(i + 2)
        if i >= 3:
            part1_second(i - 3)
        if i == 5:
            part2_second(0)
    arrive("xh0", p0_half.at[0])
    xref(0, 1)[...] = add(xref(0, 1), p0_half.at[0])
    send("xl0", xref(0, 1), p0_last.at[0, 0], xp)
    arrive("xh1", p0_half.at[1])
    xref(1, -1)[...] = add(xref(1, -1), p0_half.at[1])
    send("xl1", xref(1, -1), p0_last.at[1, 1], xm)
    part1_second(5)
    part2_second(1)
    part2_second(2)

    for j in range(1, group):
        arrive(f"a{j}", arrived.at[lax.rem(me + group - j, group)])
    for s in range(slots):
        source = recv_from[s]
        kept = delta[pl.ds(s * tokens, tokens), :]
        settled[pl.ds(s * tokens, tokens), :] = jnp.where(source == me, kept, arrived[source])
    hg_copies = []

    def back(j):
        block = w[2 * j : 2 * j + 2].reshape(span, w.shape[2])
        value = lax.dot_general(
            settled[...], block, (((1,), (1,)), ((), ())), preferred_element_type=f32
        )
        take[j] = value.astype(bf16).reshape(take.shape[1:])
        one = pltpu.make_async_copy(
            take.at[j], hg_out.at[:, :, pl.ds(j * span, span)], local_sem.at[4 + j]
        )
        one.start()
        hg_copies.append(one)

    back(0)
    part1_second(6)
    back(1)
    part2_second(3)
    part1_second(7)
    for i in range(4):
        part1_last(i)
    back(2)
    part2_last(0)
    part1_last(4)
    part1_last(5)
    back(3)
    part2_last(1)
    part2_last(2)
    back(4)
    part2_last(3)
    part1_last(6)
    part1_last(7)

    steps = ((1, xp), (-1, xm), (2, x2))
    for n, (dx, target) in enumerate(steps):
        for hh in (0, 1):
            src = summed.at[index(hh, dx), zrows(0), lanes[1]]
            send(f"s1{n}{hh}", src, p1_two.at[n, hh], target)

    def zpiece(dz):
        lower = pl.ds(pl.multiple_of(256 + l * 128 + wrap(z + dz) * 32, 32), 32)
        return summed.at[pl.ds(pl.multiple_of(h * 4, 4), 4), lower, lanes[2]]

    for n, (dz, target) in enumerate(((1, zp), (-1, zm), (2, z2))):
        send(f"s2{n}", zpiece(dz), p2_two.at[n], target)
    for hh in (0, 1):
        arrive(f"xn{hh}", p0_last.at[1 - hh, hh])
        arrive(f"xl{hh}", p0_last.at[hh, hh])
        xref(hh, 0)[...] = add(xref(hh, 0), p0_last.at[0, hh], p0_last.at[1, hh])

    def ypiece(dy):
        q = wrap(y + dy)
        some = pl.ds(pl.multiple_of(lax.rem(q, 2) * 256, 256), 256)
        return summed.at[lax.div(q, 2) * 4 + x, some, lanes[0]]

    for n, (dy, target) in enumerate(((1, yp), (-1, ym), (2, y2))):
        send(f"s0{n}", ypiece(dy), p0_two.at[n], target)
    back(5)
    for n in range(3):
        arrive(f"s2{n}", p2_two.at[n])
    zpiece(0)[...] = add(zpiece(0), p2_two.at[0], p2_two.at[1], p2_two.at[2])

    piece_rows = pl.ds(pl.multiple_of(256 + l * 128 + z * 32, 32), 32)
    for n, (dx, target) in enumerate(steps):
        send(f"t2{n}", summed.at[index(h, dx), piece_rows, lanes[2]], p2_three.at[n], target)
    back(6)
    for n in range(3):
        for hh in (0, 1):
            arrive(f"s1{n}{hh}", p1_two.at[n, hh])
    for hh in (0, 1):
        ref = summed.at[index(hh, 0), zrows(0), lanes[1]]
        ref[...] = add(ref, p1_two.at[0, hh], p1_two.at[1, hh], p1_two.at[2, hh])

    def third1(dy):
        q = wrap(y + dy)
        some = pl.ds(pl.multiple_of(z * 64 + lax.rem(q, 2) * 32, 32), 32)
        return summed.at[lax.div(q, 2) * 4 + x, some, lanes[1]]

    for n, (dy, target) in enumerate(((1, yp), (-1, ym), (2, y2))):
        send(f"t1{n}", third1(dy), p1_three.at[n], target)
    back(7)
    for n in range(3):
        arrive(f"s0{n}", p0_two.at[n])
    ypiece(0)[...] = add(ypiece(0), p0_two.at[0], p0_two.at[1], p0_two.at[2])

    def third0(dz):
        some = pl.ds(pl.multiple_of(l * 256 + wrap(z + dz) * 64, 64), 64)
        return summed.at[h * 4 + x, some, lanes[0]]

    for n, (dz, target) in enumerate(((1, zp), (-1, zm), (2, z2))):
        send(f"t0{n}", third0(dz), p0_three.at[n], target)

    def finish(part, ref, buffer):
        for n in range(3):
            arrive(f"t{part}{n}", buffer.at[n])
        value = add(ref, buffer.at[0], buffer.at[1], buffer.at[2])
        mine = done.at[c, l, z, rest[part], lanes[part]]
        mine[...] = value
        send(f"gy{part}", mine, mine, twin)
        send(f"gp{part}", mine, mine, zp)
        send(f"gm{part}", mine, mine, zm)
        send(f"g2{part}", mine, mine, z2)

    def pass_on(part):
        def piece(ll, dz):
            return done.at[c, ll, wrap(z + dz), rest[part], lanes[part]]

        arrive(f"gy{part}", piece(1 - l, 0))
        send(f"fp{part}", piece(1 - l, 0), piece(1 - l, 0), zp)
        send(f"fm{part}", piece(1 - l, 0), piece(1 - l, 0), zm)
        arrive(f"g2{part}", piece(l, 2))
        send(f"fy{part}", piece(l, 2), piece(l, 2), twin)

    def collect(part):
        def piece(ll, dz):
            return done.at[c, ll, wrap(z + dz), rest[part], lanes[part]]

        arrive(f"gp{part}", piece(l, -1))
        arrive(f"gm{part}", piece(l, 1))
        arrive(f"fp{part}", piece(1 - l, -1))
        arrive(f"fm{part}", piece(1 - l, 1))
        arrive(f"fy{part}", piece(1 - l, 2))
        ref = done.at[c, :, :, rest[part], lanes[part]]
        send(f"e{part}", ref, ref, peer)

    finish(2, summed.at[h * 4 + x, piece_rows, lanes[2]], p2_three)
    finish(1, third1(0), p1_three)
    pass_on(2)
    finish(0, third0(0), p0_three)
    pass_on(1)
    collect(2)
    pass_on(0)
    collect(1)
    collect(0)
    for part in (2, 1, 0):
        arrive(f"e{part}", done.at[1 - c, :, :, rest[part], lanes[part]])
    out_copy = pltpu.make_async_copy(done, gt_out, local_sem.at[3])
    out_copy.start()
    for one in started:
        one.wait_send()
    for one in hg_copies:
        one.wait()
    out_copy.wait()


def main_call(counts, send_peer, recv_from, key_weight, value_weight, hidden, queries, out_grad):
    rows, width = key_weight.shape
    blocks, group = lax.axis_size("fsdp"), lax.axis_size("dp")
    slots, tokens, _ = hidden.shape
    total, cols, span, chips = slots * tokens, 2 * width, 2 * rows, blocks // 2
    bf16 = jnp.bfloat16
    smem = pl.BlockSpec(memory_space=pltpu.SMEM)
    vmem = pl.BlockSpec(memory_space=pltpu.VMEM)
    hbm = pl.BlockSpec(memory_space=pl.ANY)

    def buffer(*shape):
        return pltpu.VMEM(shape, bf16)

    return pl.pallas_call(
        main_kernel,
        name="main",
        out_shape=(
            jax.ShapeDtypeStruct(hidden.shape, bf16),
            jax.ShapeDtypeStruct((2, 2, 4, width // 8, span), bf16),
        ),
        in_specs=[smem, smem, smem, vmem, vmem, hbm, hbm, hbm],
        out_specs=(hbm, hbm),
        scratch_shapes=[
            buffer(blocks, rows, cols),
            buffer(*hidden.shape),
            buffer(*queries.shape),
            buffer(*out_grad.shape),
            pltpu.VMEM((total, cols), jnp.float32),
            buffer(total, cols),
            buffer(total, cols),
            buffer(group, tokens, cols),
            buffer(group, tokens, cols),
            buffer(total, cols),
            buffer(2, width, total),
            buffer(chips, width, span),
            buffer(chips, slots, tokens, span),
            buffer(chips, slots, tokens, span),
            buffer(2, width, 256),
            buffer(2, 2, width, 256),
            buffer(8, width // 8, 384),
            buffer(2, 8, width // 8, 384),
            buffer(4, width // 4, 384),
            buffer(2, 4, width // 4, 384),
            buffer(3, width // 2, 256),
            buffer(3, 2, width // 8, 384),
            buffer(3, 4, width // 16, 384),
            buffer(3, width // 8, 256),
            buffer(3, width // 16, 384),
            buffer(3, width // 16, 384),
            buffer(2, 2, 4, width // 8, span),
            pltpu.SemaphoreType.DMA((176,)),
            pltpu.SemaphoreType.DMA((176,)),
            pltpu.SemaphoreType.DMA((12,)),
        ],
        compiler_params=pltpu.CompilerParams(
            collective_id=0, has_side_effects=True, vmem_limit_bytes=62 << 20
        ),
        cost_estimate=pl.CostEstimate(
            flops=6 * total * blocks * rows * cols, bytes_accessed=22 << 20, transcendentals=0
        ),
    )(counts, send_peer, recv_from, key_weight, value_weight, hidden, queries, out_grad)


def finish_kernel(hg_in, pieces_in, hg_out, key_grad, value_grad, hg, pieces, sem):
    chunks = 8
    step = hg.shape[0] // chunks
    first = pltpu.make_async_copy(pieces_in, pieces, sem.at[2 * chunks])
    first.start()

    def chunk(i, src, dst, offset):
        at = pl.ds(i * step, step)
        return pltpu.make_async_copy(src.at[at], dst.at[at], sem.at[offset + i])

    for i in range(chunks):
        chunk(i, hg_in, hg, 0).start()
    first.wait()
    for i in range(chunks):
        chunk(i, hg_in, hg, 0).wait()
        chunk(i, hg, hg_out, chunks).start()
    core = lax.rem(lax.axis_index("fsdp"), 2)
    rows, width = key_grad.shape
    for t, out in enumerate((key_grad, value_grad)):
        left = pieces[t, :, :, :, :256].reshape(width, 256)
        upper = [pieces[t, l, z, :32, 256:] for z in range(4) for l in range(2)]
        lower = [pieces[t, l, z, 32:, 256:] for l in range(2) for z in range(4)]
        right = jnp.concatenate(upper + lower, axis=0)
        grads = jnp.concatenate([left, right], axis=1)
        grads = grads.astype(jnp.float32)
        out[...] = jnp.where(core == 0, grads[:, :rows], grads[:, rows:]).T
    for i in range(chunks):
        chunk(i, hg, hg_out, chunks).wait()


def finish(hidden_grad, pieces):
    rows, width = pieces.shape[-1] // 2, pieces.shape[1] * pieces.shape[2] * pieces.shape[3]
    vmem = pl.BlockSpec(memory_space=pltpu.VMEM)
    hbm = pl.BlockSpec(memory_space=pl.ANY)
    grad = jax.ShapeDtypeStruct((rows, width), jnp.float32)
    return pl.pallas_call(
        finish_kernel,
        name="finish",
        out_shape=(jax.ShapeDtypeStruct(hidden_grad.shape, hidden_grad.dtype), grad, grad),
        in_specs=[hbm, hbm],
        out_specs=(hbm, vmem, vmem),
        scratch_shapes=[
            pltpu.VMEM(hidden_grad.shape, hidden_grad.dtype),
            pltpu.VMEM(pieces.shape, pieces.dtype),
            pltpu.SemaphoreType.DMA((17,)),
        ],
        compiler_params=pltpu.CompilerParams(vmem_limit_bytes=60 << 20),
    )(hidden_grad, pieces)


def body(hidden, queries, out_grad, counts, send_peer, recv_from, key_weight, value_weight):
    hidden_grad, pieces = main_call(
        counts, send_peer, recv_from, key_weight, value_weight, hidden, queries, out_grad
    )
    return finish(hidden_grad, pieces)


def solution(mesh):
    return jax.shard_map(
        body,
        mesh=mesh,
        in_specs=(
            P(("dp", "fsdp"), None, None),
            P(("dp", "fsdp"), None, None),
            P(("dp", "fsdp"), None, None),
            P(("dp", "fsdp")),
            P(("dp", "fsdp")),
            P(("dp", "fsdp")),
            P("fsdp", None),
            P("fsdp", None),
        ),
        out_specs=(P(("dp", "fsdp"), None, None), P("fsdp", None), P("fsdp", None)),
        check_vma=False,
    )
```

```python
import jax
import jax.numpy as jnp
from jax import lax
from jax.experimental import pallas as pl
from jax.experimental.pallas import tpu as pltpu
from jax.sharding import PartitionSpec as P

HD = 128
JBLK = 16
MESH = pl.DeviceIdType.MESH


def place():
    d, f = lax.axis_index("dp"), lax.axis_index("fsdp")
    return lax.rem(lax.div(f, 2), 4), lax.div(f, 8), lax.rem(d, 2), lax.div(d, 2), lax.rem(f, 2)


def device(x, h, l, z, c):
    return (z * 2 + l, (h * 4 + x) * 2 + c)


def attend(counts, queries, grads, pair, delta, group):
    f32, bf16 = jnp.float32, jnp.bfloat16
    tokens = queries.shape[1]
    n = 4 * tokens
    half = pair.shape[1] // 2
    heads = half // HD
    share = queries.shape[2] // half
    scale = HD ** (-0.5)
    at = pl.ds(pl.multiple_of(group * n, n), n)
    slots = pl.ds(group * 4, 4)
    count = [counts[group * 4 + j].astype(f32) for j in range(4)]

    def per_slot(slot):
        return jnp.where(
            slot == 0, count[0], jnp.where(slot == 1, count[1], jnp.where(slot == 2, count[2], count[3]))
        )

    row = lax.broadcasted_iota(jnp.int32, (n, HD), 0)
    own = per_slot(lax.div(row, tokens))
    weight = jnp.where(lax.rem(row, tokens).astype(f32) < own * JBLK, 1.0, 0.0) / own
    lane = lax.broadcasted_iota(jnp.int32, (tokens, share * n), 1)
    slot = lax.div(lax.rem(lane, n), tokens)
    u = lax.broadcasted_iota(jnp.int32, (tokens, share * n), 0)
    allowed = (u <= lax.rem(lane, tokens)) & (u.astype(f32) < per_slot(slot) * JBLK)

    def fold(wide):
        a, b, c, d = (wide[j * tokens : (j + 1) * tokens] for j in range(4))
        return jnp.where(slot == 0, a, jnp.where(slot == 1, b, jnp.where(slot == 2, c, d)))

    def spread(narrow):
        parts = [jnp.where(slot == j, narrow, 0.0) for j in range(4)]
        return jnp.concatenate(parts, axis=0).astype(bf16)

    def across(a, b):
        return lax.dot_general(a, b, (((1,), (1,)), ((), ())), preferred_element_type=f32)

    for g in range(heads):
        cols = [slice((g * share + r) * HD, (g * share + r + 1) * HD) for r in range(share)]
        q = jnp.concatenate([queries[slots, :, c].reshape(n, HD) for c in cols], axis=0)
        od = jnp.concatenate(
            [(grads[slots, :, c].reshape(n, HD).astype(f32) * weight).astype(bf16) for c in cols],
            axis=0,
        )
        key = pair[at, g * HD : (g + 1) * HD]
        value = pair[at, half + g * HD : half + (g + 1) * HD]
        scores = jnp.where(allowed, fold(across(key, q)) * scale, -1e30)
        terms = jnp.exp(scores - jnp.max(scores, axis=0, keepdims=True))
        probs = terms / jnp.sum(terms, axis=0, keepdims=True)
        probs_half = probs.astype(bf16).astype(f32)
        prob_delta = fold(across(value, od))
        row_delta = jnp.sum(probs_half * prob_delta, axis=0, keepdims=True)
        score_delta = probs * (prob_delta - row_delta) * scale
        key_delta = jnp.dot(spread(score_delta), q, preferred_element_type=f32)
        value_delta = jnp.dot(spread(probs_half), od, preferred_element_type=f32)
        delta[at, g * HD : (g + 1) * HD] = key_delta.astype(bf16)
        delta[at, half + g * HD : half + (g + 1) * HD] = value_delta.astype(bf16)


def main_kernel(
    counts, send_peer, recv_from, kw, vw, hidden, queries, out_grad, hg_out, gt_out,
    w, hid, qs, gs, acc, pair, delta, leaving, arrived, settled, dt, summed, give, take,
    p0_half, p0_last, p1_half, p1_last, p2_half, p2_last,
    p0_two, p1_two, p2_two, p0_three, p1_three, p2_three, done,
    send_sem, recv_sem, local_sem,
):
    x, h, l, z, c = place()
    me, f = lax.axis_index("dp"), lax.axis_index("fsdp")
    group = lax.axis_size("dp")
    y = 2 * h + l
    rows, width = kw.shape
    cols = 2 * width
    quarter = rows // 4
    half = width
    span = 2 * rows
    slots, tokens, _ = hidden.shape
    total = slots * tokens
    f32, bf16 = jnp.float32, jnp.bfloat16

    def wrap(v):
        return lax.rem(v + 4, 4)

    def at(dx=0, dy=0, dz=0, core=c):
        q = wrap(y + dy)
        return device(wrap(x + dx), lax.div(q, 2), lax.rem(q, 2), wrap(z + dz), core)

    xp, xm, x2 = at(dx=1), at(dx=-1), at(dx=2)
    yp, ym, y2 = at(dy=1), at(dy=-1), at(dy=2)
    zp, zm, z2 = at(dz=1), at(dz=-1), at(dz=2)
    peer = at(core=1 - c)
    twin, yo = device(x, h, 1 - l, z, c), device(x, 1 - h, 1 - l, z, c)

    others = [(lax.rem(me + j, group), f) for j in range(1, group)]
    others += [xp, xm, x2, yo, y2, peer]
    barrier = pltpu.get_barrier_semaphore()
    for other in others:
        pl.semaphore_signal(barrier, inc=1, device_id=other, device_id_type=MESH)
    own = (h * 4 + x) * 2 + c
    shards = []
    for i, shard in enumerate((kw, vw)):
        dst = w.at[own, :, pl.ds(i * width, width)]
        shards.append(pltpu.make_async_copy(shard, dst, local_sem.at[4 + i]))
        shards[-1].start()
    for one in shards:
        one.wait()
    loads = []
    for i, (src, dst) in enumerate(((hidden, hid), (queries, qs), (out_grad, gs))):
        loads.append(pltpu.make_async_copy(src, dst, local_sem.at[i]))
        loads[-1].start()
    hid_copy = loads[0]
    pl.semaphore_wait(barrier, len(others))

    number = {}
    started = []

    def copy(name, src, dst, target):
        i = number.setdefault(name, len(number))
        return pltpu.make_async_remote_copy(
            src_ref=src, dst_ref=dst, send_sem=send_sem.at[i], recv_sem=recv_sem.at[i],
            device_id=target, device_id_type=MESH,
        )

    def send(name, src, dst, target):
        one = copy(name, src, dst, target)
        one.start()
        started.append(one)

    def arrive(name, dst):
        copy(name, dst, dst, peer).wait_recv()

    def w_send(name, block, row, col, target):
        ref = w.at[block, pl.ds(*row), pl.ds(*col)]
        send(name, ref, ref, target)

    def w_arrive(name, block, row, col):
        arrive(name, w.at[block, pl.ds(*row), pl.ds(*col)])

    shared, paired, direct, wide = (512, 512), (256, 256), (0, 256), (0, 512)
    shared_cut = ((512, 256), (768, 256))
    paired_cut = ((256, 128), (384, 128))
    whole, low, high = (0, rows), (0, rows // 2), (rows // 2, rows // 2)
    my_rows = (pl.multiple_of(l * (rows // 2), rows // 2), rows // 2)
    twin_rows = (pl.multiple_of((1 - l) * (rows // 2), rows // 2), rows // 2)
    blocks_in = [(1, 0), (0, -1), (0, 1), (1, -1), (1, 1), (0, 2), (1, 2)]
    side = (h, 1 - h)

    def block(hh, dx, core=c):
        return (hh * 4 + wrap(x + dx)) * 2 + core

    def source(b, core=c):
        return block(side[blocks_in[b][0]], blocks_in[b][1], core)

    def part(dz):
        return (pl.multiple_of(wrap(z + dz) * quarter, quarter), quarter)

    def along_z(b):
        w_send(f"zp{b}", source(b), part(0), shared, zp)
        w_send(f"zm{b}", source(b), part(0), shared, zm)

    def forward_z(b):
        w_arrive(f"zp{b}", source(b), part(-1), shared)
        w_send(f"zfp{b}", source(b), part(-1), shared_cut[0], zp)
        w_arrive(f"zm{b}", source(b), part(1), shared)
        w_send(f"zfm{b}", source(b), part(1), shared_cut[1], zm)

    def finish_z(b):
        w_arrive(f"zfp{b}", source(b), part(2), shared_cut[0])
        w_arrive(f"zfm{b}", source(b), part(2), shared_cut[1])
        w_send(f"pc{b}", source(b), whole, shared, peer)

    def finish_wide(b):
        w_arrive(f"td{b}", source(b), twin_rows, paired)
        if b in (0, 3, 4, 6):
            w_arrive(f"by{b}", source(b), whole, direct)
        w_send(f"pa{b}", source(b), whole, wide, peer)

    def to_twin(b):
        w_send(f"td{b}", source(b), my_rows, paired, twin)

    def project(b):
        if b < 0:
            w_arrive("own", block(h, 0, 1 - c), whole, (0, cols))
            k = h * 4 + x
        else:
            w_arrive(f"pa{b}", source(b, 1 - c), whole, wide)
            w_arrive(f"pc{b}", source(b, 1 - c), whole, shared)
            k = side[blocks_in[b][0]] * 4 + wrap(x + blocks_in[b][1])
        left = pl.ds(pl.multiple_of(k * span, 128), span)
        right = pl.ds(pl.multiple_of(k * 2, 2), 2)

        @pl.loop(0, cols // 256)
        def _(n):
            at = pl.ds(pl.multiple_of(n * 256, 256), 256)
            value = jnp.dot(
                hid[:, :, left].reshape(total, span),
                w[right, :, at].reshape(span, 256),
                preferred_element_type=jnp.float32,
            )
            if b < 0:
                acc[:, at] = value
            elif b < 6:
                acc[:, at] += value
            else:
                pair[:, at] = (acc[:, at] + value).astype(jnp.bfloat16)

    w_send("cy", own, part(0), shared, yo)
    w_send("cxp0", own, part(0), shared, xp)
    w_send("cxm0", own, part(0), shared, xm)
    w_send("dy", own, twin_rows, paired, yo)
    w_send("bxp", own, whole, direct, xp)
    w_send("bxm", own, whole, direct, xm)
    w_send("by0", own, whole, direct, yo)
    w_send("own", own, whole, (0, cols), peer)

    w_arrive("cy", source(0), part(0), shared)
    w_send("cxp1", source(0), part(0), shared, xp)
    w_send("cxm1", source(0), part(0), shared, xm)
    along_z(0)
    w_arrive("cxp0", source(1), part(0), shared)
    w_send("cfp0", source(1), part(0), shared_cut[0], xp)
    along_z(1)
    w_arrive("cxm0", source(2), part(0), shared)
    w_send("cfm0", source(2), part(0), shared_cut[1], xm)
    along_z(2)
    w_send("dxp0", own, my_rows, paired, xp)
    w_send("dxm0", own, my_rows, paired, xm)
    w_arrive("dy", source(0), my_rows, paired)
    to_twin(0)
    w_arrive("cxp1", source(3), part(0), shared)
    w_send("cfp1", source(3), part(0), shared_cut[0], xp)
    w_arrive("cxm1", source(4), part(0), shared)
    w_send("cfm1", source(4), part(0), shared_cut[1], xm)
    w_send("dxp1", source(0), my_rows, paired, xp)
    w_send("dxm1", source(0), my_rows, paired, xm)
    forward_z(0)
    along_z(3)
    w_arrive("bxp", source(1), whole, direct)
    w_send("by3", source(1), whole, direct, yo)
    w_send("bfp", source(1), low, direct, xp)
    w_arrive("bxm", source(2), whole, direct)
    w_send("by4", source(2), whole, direct, yo)
    w_send("bfm", source(2), high, direct, xm)
    forward_z(1)
    along_z(4)
    hid_copy.wait()
    project(-1)
    for s in (0, 1):
        w_arrive(f"cfp{s}", source(5 + s), part(0), shared_cut[0])
        w_arrive(f"cfm{s}", source(5 + s), part(0), shared_cut[1])
    forward_z(2)
    along_z(5)
    for s in (0, 1):
        up, down = source(1 + 2 * s), source(2 + 2 * s)
        w_arrive(f"dxp{s}", up, my_rows, paired)
        w_send(f"dfp{s}", up, my_rows, paired_cut[0], xp)
        to_twin(1 + 2 * s)
        w_arrive(f"dxm{s}", down, my_rows, paired)
        w_send(f"dfm{s}", down, my_rows, paired_cut[1], xm)
        to_twin(2 + 2 * s)
    forward_z(3)
    along_z(6)
    w_arrive("bfp", source(5), low, direct)
    w_arrive("bfm", source(5), high, direct)
    w_send("by6", source(5), whole, direct, yo)
    for s in (0, 1):
        w_arrive(f"dfp{s}", source(5 + s), my_rows, paired_cut[0])
        w_arrive(f"dfm{s}", source(5 + s), my_rows, paired_cut[1])
        to_twin(5 + s)
    finish_wide(0)
    finish_z(0)
    forward_z(4)
    finish_wide(1)
    finish_z(1)
    project(0)
    forward_z(5)
    finish_wide(2)
    finish_z(2)
    project(1)
    forward_z(6)
    finish_wide(3)
    finish_z(3)
    project(2)
    for b in (4, 5, 6):
        finish_wide(b)
        finish_z(b)
        project(b - 1)
    project(6)

    loads[1].wait()
    loads[2].wait()

    @pl.loop(0, slots // 4)
    def _(four):
        attend(counts, qs, gs, pair, delta, four)

    def add(*refs):
        value = refs[0][...].astype(f32)
        for ref in refs[1:]:
            value = value + ref[...].astype(f32)
        return value.astype(bf16)

    def leave():
        arrived[me] = jnp.zeros(arrived.shape[1:], bf16)
        for j in range(1, group):
            to = lax.rem(me + j, group)
            chosen = delta[pl.ds(0, tokens), :]
            for s in range(1, slots):
                here = delta[pl.ds(s * tokens, tokens), :]
                chosen = jnp.where(send_peer[s] == to, here, chosen)
            leaving[to] = chosen
            send(f"a{j}", leaving.at[to], arrived.at[me], (to, f))

    def turn(t):
        dt[t] = delta[:, pl.ds(pl.multiple_of(t * half, half), half)].T

    lanes = (pl.ds(0, 256), pl.ds(256, 384), pl.ds(256, 384))
    rest = (pl.ds(0, 64), pl.ds(0, 32), pl.ds(32, 32))
    order = [(0, 2), (1, 2), (1, 1), (0, -1), (0, 1), (1, -1), (0, 0), (1, 0)]

    def index(hh, dx):
        return hh * 4 + wrap(x + dx)

    def term(t, k):
        cut = pl.ds(pl.multiple_of(k * span, 128), span)
        return jnp.dot(dt[t], hid[:, :, cut].reshape(total, span), preferred_element_type=f32)

    def other_half(i):
        k = index(*order[i])
        give[k] = term(1 - c, k).astype(bf16).reshape(give.shape[1:])
        send(f"d{i}", give.at[k], take.at[k], peer)

    def own_half(i):
        k = index(*order[i])
        value = term(c, k)
        arrive(f"d{i}", take.at[k])
        summed[k] = (value + take[k].reshape(value.shape).astype(f32)).astype(bf16)

    def zrows(dz):
        return pl.ds(pl.multiple_of(wrap(z + dz) * 64, 64), 64)

    def part1_first(i):
        k = index(*order[i])
        up, down = (2, -1) if i % 2 == 0 else (1, 2)
        one, two = ("h", "n") if i % 2 == 0 else ("n", "h")
        far_dst, near_dst = p1_half.at[i], p1_last.at[1 if i % 2 == 0 else 0, i]
        dst = {"h": far_dst, "n": near_dst}
        send(f"z{one}{i}", summed.at[k, zrows(up), lanes[1]], dst[one], zp)
        send(f"z{two}{i}", summed.at[k, zrows(down), lanes[1]], dst[two], zm)

    def part1_second(i):
        k = index(*order[i])
        near, target = (1, zp) if i % 2 == 0 else (-1, zm)
        arrive(f"zh{i}", p1_half.at[i])
        ref = summed.at[k, zrows(near), lanes[1]]
        ref[...] = add(ref, p1_half.at[i])
        send(f"zl{i}", ref, p1_last.at[0 if i % 2 == 0 else 1, i], target)

    def part1_last(i):
        k = index(*order[i])
        arrive(f"zn{i}", p1_last.at[1 if i % 2 == 0 else 0, i])
        arrive(f"zl{i}", p1_last.at[0 if i % 2 == 0 else 1, i])
        ref = summed.at[k, zrows(0), lanes[1]]
        ref[...] = add(ref, p1_last.at[0, i], p1_last.at[1, i])

    def yref(dy, dx):
        q = wrap(y + dy)
        lower = pl.ds(pl.multiple_of(256 + lax.rem(q, 2) * 128, 128), 128)
        return summed.at[lax.div(q, 2) * 4 + wrap(x + dx), lower, lanes[2]]

    shifts = (2, 1, -1, 0)

    def part2_first(j):
        dx = shifts[j]
        if j % 2 == 0:
            send(f"yh{j}", yref(2, dx), p2_half.at[j], yp)
            send(f"yn{j}", yref(-1, dx), p2_last.at[1, j], ym)
        else:
            send(f"yn{j}", yref(1, dx), p2_last.at[0, j], yp)
            send(f"yh{j}", yref(2, dx), p2_half.at[j], ym)

    def part2_second(j):
        near, target = (1, yp) if j % 2 == 0 else (-1, ym)
        arrive(f"yh{j}", p2_half.at[j])
        ref = yref(near, shifts[j])
        ref[...] = add(ref, p2_half.at[j])
        send(f"yl{j}", ref, p2_last.at[0 if j % 2 == 0 else 1, j], target)

    def part2_last(j):
        arrive(f"yn{j}", p2_last.at[1 if j % 2 == 0 else 0, j])
        arrive(f"yl{j}", p2_last.at[0 if j % 2 == 0 else 1, j])
        ref = yref(0, shifts[j])
        ref[...] = add(ref, p2_last.at[0, j], p2_last.at[1, j])

    def xref(hh, dx):
        return summed.at[index(hh, dx), :, lanes[0]]

    turn(1 - c)
    other_half(0)
    leave()
    other_half(1)
    turn(c)
    for i in range(8):
        own_half(i)
        if i == 0:
            send("xh0", xref(0, 2), p0_half.at[0], xp)
        elif i == 1:
            send("xh1", xref(1, 2), p0_half.at[1], xm)
        elif i == 2:
            send("xn1", xref(1, 1), p0_last.at[0, 1], xp)
        elif i == 3:
            send("xn0", xref(0, -1), p0_last.at[1, 0], xm)
        part1_first(i)
        if i == 1:
            part2_first(0)
        elif i == 5:
            part2_first(1)
            part2_first(2)
        elif i == 7:
            part2_first(3)
        if i + 2 < 8:
            other_half(i + 2)
        if i >= 3:
            part1_second(i - 3)
        if i == 5:
            part2_second(0)
    arrive("xh0", p0_half.at[0])
    xref(0, 1)[...] = add(xref(0, 1), p0_half.at[0])
    send("xl0", xref(0, 1), p0_last.at[0, 0], xp)
    arrive("xh1", p0_half.at[1])
    xref(1, -1)[...] = add(xref(1, -1), p0_half.at[1])
    send("xl1", xref(1, -1), p0_last.at[1, 1], xm)
    part1_second(5)
    part2_second(1)
    part2_second(2)

    for j in range(1, group):
        arrive(f"a{j}", arrived.at[lax.rem(me + group - j, group)])
    for s in range(slots):
        source = recv_from[s]
        kept = delta[pl.ds(s * tokens, tokens), :]
        settled[pl.ds(s * tokens, tokens), :] = jnp.where(source == me, kept, arrived[source])
    hg_copies = []

    def back(j):
        block = w[2 * j : 2 * j + 2].reshape(span, w.shape[2])
        value = lax.dot_general(
            settled[...], block, (((1,), (1,)), ((), ())), preferred_element_type=f32
        )
        take[j] = value.astype(bf16).reshape(take.shape[1:])
        one = pltpu.make_async_copy(
            take.at[j], hg_out.at[:, :, pl.ds(j * span, span)], local_sem.at[4 + j]
        )
        one.start()
        hg_copies.append(one)

    back(0)
    part1_second(6)
    back(1)
    part2_second(3)
    part1_second(7)
    for i in range(4):
        part1_last(i)
    back(2)
    part2_last(0)
    part1_last(4)
    part1_last(5)
    back(3)
    part2_last(1)
    part2_last(2)
    back(4)
    part2_last(3)
    part1_last(6)
    part1_last(7)

    steps = ((1, xp), (-1, xm), (2, x2))
    for n, (dx, target) in enumerate(steps):
        for hh in (0, 1):
            src = summed.at[index(hh, dx), zrows(0), lanes[1]]
            send(f"s1{n}{hh}", src, p1_two.at[n, hh], target)

    def zpiece(dz):
        lower = pl.ds(pl.multiple_of(256 + l * 128 + wrap(z + dz) * 32, 32), 32)
        return summed.at[pl.ds(pl.multiple_of(h * 4, 4), 4), lower, lanes[2]]

    for n, (dz, target) in enumerate(((1, zp), (-1, zm), (2, z2))):
        send(f"s2{n}", zpiece(dz), p2_two.at[n], target)
    for hh in (0, 1):
        arrive(f"xn{hh}", p0_last.at[1 - hh, hh])
        arrive(f"xl{hh}", p0_last.at[hh, hh])
        xref(hh, 0)[...] = add(xref(hh, 0), p0_last.at[0, hh], p0_last.at[1, hh])

    def ypiece(dy):
        q = wrap(y + dy)
        some = pl.ds(pl.multiple_of(lax.rem(q, 2) * 256, 256), 256)
        return summed.at[lax.div(q, 2) * 4 + x, some, lanes[0]]

    for n, (dy, target) in enumerate(((1, yp), (-1, ym), (2, y2))):
        send(f"s0{n}", ypiece(dy), p0_two.at[n], target)
    back(5)
    for n in range(3):
        arrive(f"s2{n}", p2_two.at[n])
    zpiece(0)[...] = add(zpiece(0), p2_two.at[0], p2_two.at[1], p2_two.at[2])

    piece_rows = pl.ds(pl.multiple_of(256 + l * 128 + z * 32, 32), 32)
    for n, (dx, target) in enumerate(steps):
        send(f"t2{n}", summed.at[index(h, dx), piece_rows, lanes[2]], p2_three.at[n], target)
    back(6)
    for n in range(3):
        for hh in (0, 1):
            arrive(f"s1{n}{hh}", p1_two.at[n, hh])
    for hh in (0, 1):
        ref = summed.at[index(hh, 0), zrows(0), lanes[1]]
        ref[...] = add(ref, p1_two.at[0, hh], p1_two.at[1, hh], p1_two.at[2, hh])

    def third1(dy):
        q = wrap(y + dy)
        some = pl.ds(pl.multiple_of(z * 64 + lax.rem(q, 2) * 32, 32), 32)
        return summed.at[lax.div(q, 2) * 4 + x, some, lanes[1]]

    for n, (dy, target) in enumerate(((1, yp), (-1, ym), (2, y2))):
        send(f"t1{n}", third1(dy), p1_three.at[n], target)
    back(7)
    for n in range(3):
        arrive(f"s0{n}", p0_two.at[n])
    ypiece(0)[...] = add(ypiece(0), p0_two.at[0], p0_two.at[1], p0_two.at[2])

    def third0(dz):
        some = pl.ds(pl.multiple_of(l * 256 + wrap(z + dz) * 64, 64), 64)
        return summed.at[h * 4 + x, some, lanes[0]]

    for n, (dz, target) in enumerate(((1, zp), (-1, zm), (2, z2))):
        send(f"t0{n}", third0(dz), p0_three.at[n], target)

    def finish(part, ref, buffer):
        for n in range(3):
            arrive(f"t{part}{n}", buffer.at[n])
        value = add(ref, buffer.at[0], buffer.at[1], buffer.at[2])
        mine = done.at[c, l, z, rest[part], lanes[part]]
        mine[...] = value
        send(f"gy{part}", mine, mine, twin)
        send(f"gp{part}", mine, mine, zp)
        send(f"gm{part}", mine, mine, zm)
        send(f"g2{part}", mine, mine, z2)

    def pass_on(part):
        def piece(ll, dz):
            return done.at[c, ll, wrap(z + dz), rest[part], lanes[part]]

        arrive(f"gy{part}", piece(1 - l, 0))
        send(f"fp{part}", piece(1 - l, 0), piece(1 - l, 0), zp)
        send(f"fm{part}", piece(1 - l, 0), piece(1 - l, 0), zm)
        arrive(f"g2{part}", piece(l, 2))
        send(f"fy{part}", piece(l, 2), piece(l, 2), twin)

    def collect(part):
        def piece(ll, dz):
            return done.at[c, ll, wrap(z + dz), rest[part], lanes[part]]

        arrive(f"gp{part}", piece(l, -1))
        arrive(f"gm{part}", piece(l, 1))
        arrive(f"fp{part}", piece(1 - l, -1))
        arrive(f"fm{part}", piece(1 - l, 1))
        arrive(f"fy{part}", piece(1 - l, 2))
        ref = done.at[c, :, :, rest[part], lanes[part]]
        send(f"e{part}", ref, ref, peer)

    finish(2, summed.at[h * 4 + x, piece_rows, lanes[2]], p2_three)
    finish(1, third1(0), p1_three)
    pass_on(2)
    finish(0, third0(0), p0_three)
    pass_on(1)
    collect(2)
    pass_on(0)
    collect(1)
    collect(0)
    for part in (2, 1, 0):
        arrive(f"e{part}", done.at[1 - c, :, :, rest[part], lanes[part]])
    out_copy = pltpu.make_async_copy(done, gt_out, local_sem.at[3])
    out_copy.start()
    for one in started:
        one.wait_send()
    for one in hg_copies:
        one.wait()
    out_copy.wait()


def main_call(counts, send_peer, recv_from, key_weight, value_weight, hidden, queries, out_grad):
    rows, width = key_weight.shape
    blocks, group = lax.axis_size("fsdp"), lax.axis_size("dp")
    slots, tokens, _ = hidden.shape
    total, cols, span, chips = slots * tokens, 2 * width, 2 * rows, blocks // 2
    bf16 = jnp.bfloat16
    smem = pl.BlockSpec(memory_space=pltpu.SMEM)
    hbm = pl.BlockSpec(memory_space=pl.ANY)

    def buffer(*shape):
        return pltpu.VMEM(shape, bf16)

    return pl.pallas_call(
        main_kernel,
        name="main",
        out_shape=(
            jax.ShapeDtypeStruct(hidden.shape, bf16),
            jax.ShapeDtypeStruct((2, 2, 4, width // 8, span), bf16),
        ),
        in_specs=[smem, smem, smem, hbm, hbm, hbm, hbm, hbm],
        out_specs=(hbm, hbm),
        scratch_shapes=[
            buffer(blocks, rows, cols),
            buffer(*hidden.shape),
            buffer(*queries.shape),
            buffer(*out_grad.shape),
            pltpu.VMEM((total, cols), jnp.float32),
            buffer(total, cols),
            buffer(total, cols),
            buffer(group, tokens, cols),
            buffer(group, tokens, cols),
            buffer(total, cols),
            buffer(2, width, total),
            buffer(chips, width, span),
            buffer(chips, slots, tokens, span),
            buffer(chips, slots, tokens, span),
            buffer(2, width, 256),
            buffer(2, 2, width, 256),
            buffer(8, width // 8, 384),
            buffer(2, 8, width // 8, 384),
            buffer(4, width // 4, 384),
            buffer(2, 4, width // 4, 384),
            buffer(3, width // 2, 256),
            buffer(3, 2, width // 8, 384),
            buffer(3, 4, width // 16, 384),
            buffer(3, width // 8, 256),
            buffer(3, width // 16, 384),
            buffer(3, width // 16, 384),
            buffer(2, 2, 4, width // 8, span),
            pltpu.SemaphoreType.DMA((192,)),
            pltpu.SemaphoreType.DMA((192,)),
            pltpu.SemaphoreType.DMA((12,)),
        ],
        compiler_params=pltpu.CompilerParams(
            collective_id=0, has_side_effects=True, vmem_limit_bytes=62 << 20
        ),
        cost_estimate=pl.CostEstimate(
            flops=6 * total * blocks * rows * cols, bytes_accessed=22 << 20, transcendentals=0
        ),
    )(counts, send_peer, recv_from, key_weight, value_weight, hidden, queries, out_grad)


def finish_kernel(hg_in, pieces_in, hg_out, key_grad, value_grad, hg, pieces, sem):
    chunks = 8
    step = hg.shape[0] // chunks
    first = pltpu.make_async_copy(pieces_in, pieces, sem.at[2 * chunks])
    first.start()

    def chunk(i, src, dst, offset):
        at = pl.ds(i * step, step)
        return pltpu.make_async_copy(src.at[at], dst.at[at], sem.at[offset + i])

    for i in range(chunks):
        chunk(i, hg_in, hg, 0).start()
    first.wait()
    for i in range(chunks):
        chunk(i, hg_in, hg, 0).wait()
        chunk(i, hg, hg_out, chunks).start()
    core = lax.rem(lax.axis_index("fsdp"), 2)
    rows, width = key_grad.shape
    for t, out in enumerate((key_grad, value_grad)):
        left = pieces[t, :, :, :, :256].reshape(width, 256)
        upper = [pieces[t, l, z, :32, 256:] for z in range(4) for l in range(2)]
        lower = [pieces[t, l, z, 32:, 256:] for l in range(2) for z in range(4)]
        right = jnp.concatenate(upper + lower, axis=0)
        grads = jnp.concatenate([left, right], axis=1)
        grads = grads.astype(jnp.float32)
        out[...] = jnp.where(core == 0, grads[:, :rows], grads[:, rows:]).T
    for i in range(chunks):
        chunk(i, hg, hg_out, chunks).wait()


def finish(hidden_grad, pieces):
    rows, width = pieces.shape[-1] // 2, pieces.shape[1] * pieces.shape[2] * pieces.shape[3]
    vmem = pl.BlockSpec(memory_space=pltpu.VMEM)
    hbm = pl.BlockSpec(memory_space=pl.ANY)
    grad = jax.ShapeDtypeStruct((rows, width), jnp.float32)
    return pl.pallas_call(
        finish_kernel,
        name="finish",
        out_shape=(jax.ShapeDtypeStruct(hidden_grad.shape, hidden_grad.dtype), grad, grad),
        in_specs=[hbm, hbm],
        out_specs=(hbm, vmem, vmem),
        scratch_shapes=[
            pltpu.VMEM(hidden_grad.shape, hidden_grad.dtype),
            pltpu.VMEM(pieces.shape, pieces.dtype),
            pltpu.SemaphoreType.DMA((17,)),
        ],
        compiler_params=pltpu.CompilerParams(vmem_limit_bytes=60 << 20),
    )(hidden_grad, pieces)


def body(hidden, queries, out_grad, counts, send_peer, recv_from, key_weight, value_weight):
    hidden_grad, pieces = main_call(
        counts, send_peer, recv_from, key_weight, value_weight, hidden, queries, out_grad
    )
    return finish(hidden_grad, pieces)


def solution(mesh):
    return jax.shard_map(
        body,
        mesh=mesh,
        in_specs=(
            P(("dp", "fsdp"), None, None),
            P(("dp", "fsdp"), None, None),
            P(("dp", "fsdp"), None, None),
            P(("dp", "fsdp")),
            P(("dp", "fsdp")),
            P(("dp", "fsdp")),
            P("fsdp", None),
            P("fsdp", None),
        ),
        out_specs=(P(("dp", "fsdp"), None, None), P("fsdp", None), P("fsdp", None)),
        check_vma=False,
    )
```

```python
import jax
import jax.numpy as jnp
from jax import lax
from jax.experimental import pallas as pl
from jax.experimental.pallas import tpu as pltpu
from jax.sharding import PartitionSpec as P

HD = 128
JBLK = 16
MESH = pl.DeviceIdType.MESH


def place():
    d, f = lax.axis_index("dp"), lax.axis_index("fsdp")
    return lax.rem(lax.div(f, 2), 4), lax.div(f, 8), lax.rem(d, 2), lax.div(d, 2), lax.rem(f, 2)


def device(x, h, l, z, c):
    return (z * 2 + l, (h * 4 + x) * 2 + c)


def attend(counts, queries, grads, pair, delta, group):
    f32, bf16 = jnp.float32, jnp.bfloat16
    tokens = queries.shape[1]
    n = 4 * tokens
    half = pair.shape[1] // 2
    heads = half // HD
    share = queries.shape[2] // half
    scale = HD ** (-0.5)
    at = pl.ds(pl.multiple_of(group * n, n), n)
    slots = pl.ds(group * 4, 4)
    count = [counts[group * 4 + j].astype(f32) for j in range(4)]

    def per_slot(slot):
        return jnp.where(
            slot == 0, count[0], jnp.where(slot == 1, count[1], jnp.where(slot == 2, count[2], count[3]))
        )

    row = lax.broadcasted_iota(jnp.int32, (n, HD), 0)
    own = per_slot(lax.div(row, tokens))
    weight = jnp.where(lax.rem(row, tokens).astype(f32) < own * JBLK, 1.0, 0.0) / own
    lane = lax.broadcasted_iota(jnp.int32, (tokens, share * n), 1)
    slot = lax.div(lax.rem(lane, n), tokens)
    u = lax.broadcasted_iota(jnp.int32, (tokens, share * n), 0)
    allowed = (u <= lax.rem(lane, tokens)) & (u.astype(f32) < per_slot(slot) * JBLK)

    def fold(wide):
        a, b, c, d = (wide[j * tokens : (j + 1) * tokens] for j in range(4))
        return jnp.where(slot == 0, a, jnp.where(slot == 1, b, jnp.where(slot == 2, c, d)))

    def spread(narrow):
        parts = [jnp.where(slot == j, narrow, 0.0) for j in range(4)]
        return jnp.concatenate(parts, axis=0).astype(bf16)

    def across(a, b):
        return lax.dot_general(a, b, (((1,), (1,)), ((), ())), preferred_element_type=f32)

    for g in range(heads):
        cols = [slice((g * share + r) * HD, (g * share + r + 1) * HD) for r in range(share)]
        q = jnp.concatenate([queries[slots, :, c].reshape(n, HD) for c in cols], axis=0)
        od = jnp.concatenate(
            [(grads[slots, :, c].reshape(n, HD).astype(f32) * weight).astype(bf16) for c in cols],
            axis=0,
        )
        key = pair[at, g * HD : (g + 1) * HD]
        value = pair[at, half + g * HD : half + (g + 1) * HD]
        scores = jnp.where(allowed, fold(across(key, q)) * scale, -1e30)
        terms = jnp.exp(scores - jnp.max(scores, axis=0, keepdims=True))
        probs = terms / jnp.sum(terms, axis=0, keepdims=True)
        probs_half = probs.astype(bf16).astype(f32)
        prob_delta = fold(across(value, od))
        row_delta = jnp.sum(probs_half * prob_delta, axis=0, keepdims=True)
        score_delta = probs * (prob_delta - row_delta) * scale
        key_delta = jnp.dot(spread(score_delta), q, preferred_element_type=f32)
        value_delta = jnp.dot(spread(probs_half), od, preferred_element_type=f32)
        delta[at, g * HD : (g + 1) * HD] = key_delta.astype(bf16)
        delta[at, half + g * HD : half + (g + 1) * HD] = value_delta.astype(bf16)


def main_kernel(
    counts, send_peer, recv_from, kw, vw, hidden, queries, out_grad, hg_out, gt_out,
    w, hid, qs, gs, acc, pair, delta, leaving, arrived, settled, dt, summed, give, take,
    p0_half, p0_last, p1_half, p1_last, p2_half, p2_last,
    p0_two, p1_two, p2_two, p0_three, p1_three, p2_three, done,
    send_sem, recv_sem, local_sem,
):
    x, h, l, z, c = place()
    me, f = lax.axis_index("dp"), lax.axis_index("fsdp")
    group = lax.axis_size("dp")
    y = 2 * h + l
    rows, width = kw.shape
    cols = 2 * width
    quarter = rows // 4
    half = width
    span = 2 * rows
    slots, tokens, _ = hidden.shape
    total = slots * tokens
    f32, bf16 = jnp.float32, jnp.bfloat16

    def wrap(v):
        return lax.rem(v + 4, 4)

    def at(dx=0, dy=0, dz=0, core=c):
        q = wrap(y + dy)
        return device(wrap(x + dx), lax.div(q, 2), lax.rem(q, 2), wrap(z + dz), core)

    xp, xm, x2 = at(dx=1), at(dx=-1), at(dx=2)
    yp, ym, y2 = at(dy=1), at(dy=-1), at(dy=2)
    zp, zm, z2 = at(dz=1), at(dz=-1), at(dz=2)
    peer = at(core=1 - c)
    twin, yo = device(x, h, 1 - l, z, c), device(x, 1 - h, 1 - l, z, c)

    others = [(lax.rem(me + j, group), f) for j in range(1, group)]
    others += [xp, xm, x2, yo, y2, peer]
    barrier = pltpu.get_barrier_semaphore()
    for other in others:
        pl.semaphore_signal(barrier, inc=1, device_id=other, device_id_type=MESH)
    own = (h * 4 + x) * 2 + c
    shards = []
    for i, shard in enumerate((kw, vw)):
        dst = w.at[own, :, pl.ds(i * width, width)]
        shards.append(pltpu.make_async_copy(shard, dst, local_sem.at[4 + i]))
        shards[-1].start()
    for one in shards:
        one.wait()
    loads = []
    for i, (src, dst) in enumerate(((hidden, hid), (queries, qs), (out_grad, gs))):
        loads.append(pltpu.make_async_copy(src, dst, local_sem.at[i]))
        loads[-1].start()
    hid_copy = loads[0]
    pl.semaphore_wait(barrier, len(others))

    number = {}
    started = []

    def copy(name, src, dst, target):
        i = number.setdefault(name, len(number))
        return pltpu.make_async_remote_copy(
            src_ref=src, dst_ref=dst, send_sem=send_sem.at[i], recv_sem=recv_sem.at[i],
            device_id=target, device_id_type=MESH,
        )

    def send(name, src, dst, target):
        one = copy(name, src, dst, target)
        one.start()
        started.append(one)

    def arrive(name, dst):
        copy(name, dst, dst, peer).wait_recv()

    def w_send(name, block, row, col, target):
        ref = w.at[block, pl.ds(*row), pl.ds(*col)]
        send(name, ref, ref, target)

    def w_arrive(name, block, row, col):
        arrive(name, w.at[block, pl.ds(*row), pl.ds(*col)])

    shared, paired, direct, wide = (512, 512), (256, 256), (0, 256), (0, 512)
    shared_cut = ((512, 256), (768, 256))
    paired_cut = ((256, 128), (384, 128))
    whole, low, high = (0, rows), (0, rows // 2), (rows // 2, rows // 2)
    my_rows = (pl.multiple_of(l * (rows // 2), rows // 2), rows // 2)
    twin_rows = (pl.multiple_of((1 - l) * (rows // 2), rows // 2), rows // 2)
    blocks_in = [(1, 0), (0, -1), (0, 1), (1, -1), (1, 1), (0, 2), (1, 2)]
    side = (h, 1 - h)

    def block(hh, dx, core=c):
        return (hh * 4 + wrap(x + dx)) * 2 + core

    def source(b, core=c):
        return block(side[blocks_in[b][0]], blocks_in[b][1], core)

    def part(dz):
        return (pl.multiple_of(wrap(z + dz) * quarter, quarter), quarter)

    def along_z(b):
        w_send(f"zp{b}", source(b), part(0), shared, zp)
        w_send(f"zm{b}", source(b), part(0), shared, zm)

    def forward_z(b):
        w_arrive(f"zp{b}", source(b), part(-1), shared)
        w_send(f"zfp{b}", source(b), part(-1), shared_cut[0], zp)
        w_arrive(f"zm{b}", source(b), part(1), shared)
        w_send(f"zfm{b}", source(b), part(1), shared_cut[1], zm)

    def finish_z(b):
        w_arrive(f"zfp{b}", source(b), part(2), shared_cut[0])
        w_arrive(f"zfm{b}", source(b), part(2), shared_cut[1])
        w_send(f"pc{b}", source(b), whole, shared, peer)

    def finish_wide(b):
        w_arrive(f"td{b}", source(b), twin_rows, paired)
        if b in (0, 3, 4, 6):
            w_arrive(f"by{b}", source(b), whole, direct)
        w_send(f"pa{b}", source(b), whole, wide, peer)

    def to_twin(b):
        w_send(f"td{b}", source(b), my_rows, paired, twin)

    def project(b):
        if b < 0:
            w_arrive("own", block(h, 0, 1 - c), whole, (0, cols))
            k = h * 4 + x
        else:
            w_arrive(f"pa{b}", source(b, 1 - c), whole, wide)
            w_arrive(f"pc{b}", source(b, 1 - c), whole, shared)
            k = side[blocks_in[b][0]] * 4 + wrap(x + blocks_in[b][1])
        left = pl.ds(pl.multiple_of(k * span, 128), span)
        right = pl.ds(pl.multiple_of(k * 2, 2), 2)

        @pl.loop(0, cols // 256)
        def _(n):
            at = pl.ds(pl.multiple_of(n * 256, 256), 256)
            value = jnp.dot(
                hid[:, :, left].reshape(total, span),
                w[right, :, at].reshape(span, 256),
                preferred_element_type=jnp.float32,
            )
            if b < 0:
                acc[:, at] = value
            elif b < 6:
                acc[:, at] += value
            else:
                pair[:, at] = (acc[:, at] + value).astype(jnp.bfloat16)

    w_send("cy", own, part(0), shared, yo)
    w_send("cxp0", own, part(0), shared, xp)
    w_send("cxm0", own, part(0), shared, xm)
    w_send("dy", own, twin_rows, paired, yo)
    w_send("bxp", own, whole, direct, xp)
    w_send("bxm", own, whole, direct, xm)
    w_send("by0", own, whole, direct, yo)
    w_send("own", own, whole, (0, cols), peer)

    w_arrive("cy", source(0), part(0), shared)
    w_send("cxp1", source(0), part(0), shared, xp)
    w_send("cxm1", source(0), part(0), shared, xm)
    along_z(0)
    w_arrive("cxp0", source(1), part(0), shared)
    w_send("cfp0", source(1), part(0), shared_cut[0], xp)
    along_z(1)
    w_arrive("cxm0", source(2), part(0), shared)
    w_send("cfm0", source(2), part(0), shared_cut[1], xm)
    along_z(2)
    w_send("dxp0", own, my_rows, paired, xp)
    w_send("dxm0", own, my_rows, paired, xm)
    w_arrive("dy", source(0), my_rows, paired)
    to_twin(0)
    w_arrive("cxp1", source(3), part(0), shared)
    w_send("cfp1", source(3), part(0), shared_cut[0], xp)
    w_arrive("cxm1", source(4), part(0), shared)
    w_send("cfm1", source(4), part(0), shared_cut[1], xm)
    w_send("dxp1", source(0), my_rows, paired, xp)
    w_send("dxm1", source(0), my_rows, paired, xm)
    forward_z(0)
    along_z(3)
    w_arrive("bxp", source(1), whole, direct)
    w_send("by3", source(1), whole, direct, yo)
    w_send("bfp", source(1), low, direct, xp)
    w_arrive("bxm", source(2), whole, direct)
    w_send("by4", source(2), whole, direct, yo)
    w_send("bfm", source(2), high, direct, xm)
    forward_z(1)
    along_z(4)
    hid_copy.wait()
    project(-1)
    for s in (0, 1):
        w_arrive(f"cfp{s}", source(5 + s), part(0), shared_cut[0])
        w_arrive(f"cfm{s}", source(5 + s), part(0), shared_cut[1])
    forward_z(2)
    along_z(5)
    for s in (0, 1):
        up, down = source(1 + 2 * s), source(2 + 2 * s)
        w_arrive(f"dxp{s}", up, my_rows, paired)
        w_send(f"dfp{s}", up, my_rows, paired_cut[0], xp)
        to_twin(1 + 2 * s)
        w_arrive(f"dxm{s}", down, my_rows, paired)
        w_send(f"dfm{s}", down, my_rows, paired_cut[1], xm)
        to_twin(2 + 2 * s)
    forward_z(3)
    along_z(6)
    w_arrive("bfp", source(5), low, direct)
    w_arrive("bfm", source(5), high, direct)
    w_send("by6", source(5), whole, direct, yo)
    for s in (0, 1):
        w_arrive(f"dfp{s}", source(5 + s), my_rows, paired_cut[0])
        w_arrive(f"dfm{s}", source(5 + s), my_rows, paired_cut[1])
        to_twin(5 + s)
    finish_wide(0)
    finish_z(0)
    forward_z(4)
    finish_wide(1)
    finish_z(1)
    project(0)
    forward_z(5)
    finish_wide(2)
    finish_z(2)
    project(1)
    forward_z(6)
    finish_wide(3)
    finish_z(3)
    project(2)
    for b in (4, 5, 6):
        finish_wide(b)
        finish_z(b)
        project(b - 1)
    project(6)

    loads[1].wait()
    loads[2].wait()

    @pl.loop(0, slots // 4)
    def _(four):
        attend(counts, qs, gs, pair, delta, four)

    def add(*refs):
        value = refs[0][...].astype(f32)
        for ref in refs[1:]:
            value = value + ref[...].astype(f32)
        return value.astype(bf16)

    def leave():
        arrived[me] = jnp.zeros(arrived.shape[1:], bf16)
        for j in range(1, group):
            to = lax.rem(me + j, group)
            chosen = delta[pl.ds(0, tokens), :]
            for s in range(1, slots):
                here = delta[pl.ds(s * tokens, tokens), :]
                chosen = jnp.where(send_peer[s] == to, here, chosen)
            leaving[to] = chosen
            send(f"a{j}", leaving.at[to], arrived.at[me], (to, f))

    def turn(t):
        dt[t] = delta[:, pl.ds(pl.multiple_of(t * half, half), half)].T

    lanes = (pl.ds(0, 256), pl.ds(256, 384), pl.ds(256, 384))
    rest = (pl.ds(0, 64), pl.ds(0, 32), pl.ds(32, 32))
    order = [(0, 2), (1, 2), (1, 1), (0, -1), (0, 1), (1, -1), (0, 0), (1, 0)]

    def index(hh, dx):
        return hh * 4 + wrap(x + dx)

    def term(t, k):
        cut = pl.ds(pl.multiple_of(k * span, 128), span)
        return jnp.dot(dt[t], hid[:, :, cut].reshape(total, span), preferred_element_type=f32)

    def other_half(i):
        k = index(*order[i])
        give[k] = term(1 - c, k).astype(bf16).reshape(give.shape[1:])
        send(f"d{i}", give.at[k], take.at[k], peer)

    def own_half(i):
        k = index(*order[i])
        value = term(c, k)
        arrive(f"d{i}", take.at[k])
        summed[k] = (value + take[k].reshape(value.shape).astype(f32)).astype(bf16)

    def zrows(dz):
        return pl.ds(pl.multiple_of(wrap(z + dz) * 64, 64), 64)

    def part1_first(i):
        k = index(*order[i])
        up, down = (2, -1) if i % 2 == 0 else (1, 2)
        one, two = ("h", "n") if i % 2 == 0 else ("n", "h")
        far_dst, near_dst = p1_half.at[i], p1_last.at[1 if i % 2 == 0 else 0, i]
        dst = {"h": far_dst, "n": near_dst}
        send(f"z{one}{i}", summed.at[k, zrows(up), lanes[1]], dst[one], zp)
        send(f"z{two}{i}", summed.at[k, zrows(down), lanes[1]], dst[two], zm)

    def part1_second(i):
        k = index(*order[i])
        near, target = (1, zp) if i % 2 == 0 else (-1, zm)
        arrive(f"zh{i}", p1_half.at[i])
        ref = summed.at[k, zrows(near), lanes[1]]
        ref[...] = add(ref, p1_half.at[i])
        send(f"zl{i}", ref, p1_last.at[0 if i % 2 == 0 else 1, i], target)

    def part1_last(i):
        k = index(*order[i])
        arrive(f"zn{i}", p1_last.at[1 if i % 2 == 0 else 0, i])
        arrive(f"zl{i}", p1_last.at[0 if i % 2 == 0 else 1, i])
        ref = summed.at[k, zrows(0), lanes[1]]
        ref[...] = add(ref, p1_last.at[0, i], p1_last.at[1, i])

    def yref(dy, dx):
        q = wrap(y + dy)
        lower = pl.ds(pl.multiple_of(256 + lax.rem(q, 2) * 128, 128), 128)
        return summed.at[lax.div(q, 2) * 4 + wrap(x + dx), lower, lanes[2]]

    shifts = (2, 1, -1, 0)

    def part2_first(j):
        dx = shifts[j]
        if j % 2 == 0:
            send(f"yh{j}", yref(2, dx), p2_half.at[j], yp)
            send(f"yn{j}", yref(-1, dx), p2_last.at[1, j], ym)
        else:
            send(f"yn{j}", yref(1, dx), p2_last.at[0, j], yp)
            send(f"yh{j}", yref(2, dx), p2_half.at[j], ym)

    def part2_second(j):
        near, target = (1, yp) if j % 2 == 0 else (-1, ym)
        arrive(f"yh{j}", p2_half.at[j])
        ref = yref(near, shifts[j])
        ref[...] = add(ref, p2_half.at[j])
        send(f"yl{j}", ref, p2_last.at[0 if j % 2 == 0 else 1, j], target)

    def part2_last(j):
        arrive(f"yn{j}", p2_last.at[1 if j % 2 == 0 else 0, j])
        arrive(f"yl{j}", p2_last.at[0 if j % 2 == 0 else 1, j])
        ref = yref(0, shifts[j])
        ref[...] = add(ref, p2_last.at[0, j], p2_last.at[1, j])

    def xref(hh, dx):
        return summed.at[index(hh, dx), :, lanes[0]]

    leave()
    turn(1 - c)
    other_half(0)
    other_half(1)
    turn(c)
    for i in range(8):
        own_half(i)
        if i == 0:
            send("xh0", xref(0, 2), p0_half.at[0], xp)
        elif i == 1:
            send("xh1", xref(1, 2), p0_half.at[1], xm)
        elif i == 2:
            send("xn1", xref(1, 1), p0_last.at[0, 1], xp)
        elif i == 3:
            send("xn0", xref(0, -1), p0_last.at[1, 0], xm)
        part1_first(i)
        if i == 1:
            part2_first(0)
        elif i == 5:
            part2_first(1)
            part2_first(2)
        elif i == 7:
            part2_first(3)
        if i + 2 < 8:
            other_half(i + 2)
        if i >= 3:
            part1_second(i - 3)
        if i == 5:
            part2_second(0)
    arrive("xh0", p0_half.at[0])
    xref(0, 1)[...] = add(xref(0, 1), p0_half.at[0])
    send("xl0", xref(0, 1), p0_last.at[0, 0], xp)
    arrive("xh1", p0_half.at[1])
    xref(1, -1)[...] = add(xref(1, -1), p0_half.at[1])
    send("xl1", xref(1, -1), p0_last.at[1, 1], xm)
    part1_second(5)
    part2_second(1)
    part2_second(2)

    for j in range(1, group):
        arrive(f"a{j}", arrived.at[lax.rem(me + group - j, group)])
    for s in range(slots):
        source = recv_from[s]
        kept = delta[pl.ds(s * tokens, tokens), :]
        settled[pl.ds(s * tokens, tokens), :] = jnp.where(source == me, kept, arrived[source])
    hg_copies = []

    def back(j):
        block = w[2 * j : 2 * j + 2].reshape(span, w.shape[2])
        value = lax.dot_general(
            settled[...], block, (((1,), (1,)), ((), ())), preferred_element_type=f32
        )
        take[j] = value.astype(bf16).reshape(take.shape[1:])
        one = pltpu.make_async_copy(
            take.at[j], hg_out.at[:, :, pl.ds(j * span, span)], local_sem.at[4 + j]
        )
        one.start()
        hg_copies.append(one)

    back(0)
    part1_second(6)
    back(1)
    part2_second(3)
    part1_second(7)
    for i in range(4):
        part1_last(i)
    back(2)
    part2_last(0)
    part1_last(4)
    part1_last(5)
    back(3)
    part2_last(1)
    part2_last(2)
    back(4)
    part2_last(3)
    part1_last(6)
    part1_last(7)

    steps = ((1, xp), (-1, xm), (2, x2))
    for n, (dx, target) in enumerate(steps):
        for hh in (0, 1):
            src = summed.at[index(hh, dx), zrows(0), lanes[1]]
            send(f"s1{n}{hh}", src, p1_two.at[n, hh], target)

    def zpiece(dz):
        lower = pl.ds(pl.multiple_of(256 + l * 128 + wrap(z + dz) * 32, 32), 32)
        return summed.at[pl.ds(pl.multiple_of(h * 4, 4), 4), lower, lanes[2]]

    for n, (dz, target) in enumerate(((1, zp), (-1, zm), (2, z2))):
        send(f"s2{n}", zpiece(dz), p2_two.at[n], target)
    for hh in (0, 1):
        arrive(f"xn{hh}", p0_last.at[1 - hh, hh])
        arrive(f"xl{hh}", p0_last.at[hh, hh])
        xref(hh, 0)[...] = add(xref(hh, 0), p0_last.at[0, hh], p0_last.at[1, hh])

    def ypiece(dy):
        q = wrap(y + dy)
        some = pl.ds(pl.multiple_of(lax.rem(q, 2) * 256, 256), 256)
        return summed.at[lax.div(q, 2) * 4 + x, some, lanes[0]]

    for n, (dy, target) in enumerate(((1, yp), (-1, ym), (2, y2))):
        send(f"s0{n}", ypiece(dy), p0_two.at[n], target)
    back(5)
    for n in range(3):
        arrive(f"s2{n}", p2_two.at[n])
    zpiece(0)[...] = add(zpiece(0), p2_two.at[0], p2_two.at[1], p2_two.at[2])

    piece_rows = pl.ds(pl.multiple_of(256 + l * 128 + z * 32, 32), 32)
    for n, (dx, target) in enumerate(steps):
        send(f"t2{n}", summed.at[index(h, dx), piece_rows, lanes[2]], p2_three.at[n], target)
    back(6)
    for n in range(3):
        for hh in (0, 1):
            arrive(f"s1{n}{hh}", p1_two.at[n, hh])
    for hh in (0, 1):
        ref = summed.at[index(hh, 0), zrows(0), lanes[1]]
        ref[...] = add(ref, p1_two.at[0, hh], p1_two.at[1, hh], p1_two.at[2, hh])

    def third1(dy):
        q = wrap(y + dy)
        some = pl.ds(pl.multiple_of(z * 64 + lax.rem(q, 2) * 32, 32), 32)
        return summed.at[lax.div(q, 2) * 4 + x, some, lanes[1]]

    for n, (dy, target) in enumerate(((1, yp), (-1, ym), (2, y2))):
        send(f"t1{n}", third1(dy), p1_three.at[n], target)
    back(7)
    for n in range(3):
        arrive(f"s0{n}", p0_two.at[n])
    ypiece(0)[...] = add(ypiece(0), p0_two.at[0], p0_two.at[1], p0_two.at[2])

    def third0(dz):
        some = pl.ds(pl.multiple_of(l * 256 + wrap(z + dz) * 64, 64), 64)
        return summed.at[h * 4 + x, some, lanes[0]]

    for n, (dz, target) in enumerate(((1, zp), (-1, zm), (2, z2))):
        send(f"t0{n}", third0(dz), p0_three.at[n], target)

    def finish(part, ref, buffer):
        for n in range(3):
            arrive(f"t{part}{n}", buffer.at[n])
        value = add(ref, buffer.at[0], buffer.at[1], buffer.at[2])
        mine = done.at[c, l, z, rest[part], lanes[part]]
        mine[...] = value
        send(f"gy{part}", mine, mine, twin)
        send(f"gp{part}", mine, mine, zp)
        send(f"gm{part}", mine, mine, zm)
        send(f"g2{part}", mine, mine, z2)

    def pass_on(part):
        def piece(ll, dz):
            return done.at[c, ll, wrap(z + dz), rest[part], lanes[part]]

        arrive(f"gy{part}", piece(1 - l, 0))
        send(f"fp{part}", piece(1 - l, 0), piece(1 - l, 0), zp)
        send(f"fm{part}", piece(1 - l, 0), piece(1 - l, 0), zm)
        arrive(f"g2{part}", piece(l, 2))
        send(f"fy{part}", piece(l, 2), piece(l, 2), twin)

    def collect(part):
        def piece(ll, dz):
            return done.at[c, ll, wrap(z + dz), rest[part], lanes[part]]

        arrive(f"gp{part}", piece(l, -1))
        arrive(f"gm{part}", piece(l, 1))
        arrive(f"fp{part}", piece(1 - l, -1))
        arrive(f"fm{part}", piece(1 - l, 1))
        arrive(f"fy{part}", piece(1 - l, 2))
        ref = done.at[c, :, :, rest[part], lanes[part]]
        send(f"e{part}", ref, ref, peer)

    finish(2, summed.at[h * 4 + x, piece_rows, lanes[2]], p2_three)
    finish(1, third1(0), p1_three)
    pass_on(2)
    finish(0, third0(0), p0_three)
    pass_on(1)
    collect(2)
    pass_on(0)
    collect(1)
    collect(0)
    for part in (2, 1, 0):
        arrive(f"e{part}", done.at[1 - c, :, :, rest[part], lanes[part]])
    out_copy = pltpu.make_async_copy(done, gt_out, local_sem.at[3])
    out_copy.start()
    for one in started:
        one.wait_send()
    for one in hg_copies:
        one.wait()
    out_copy.wait()


def main_call(counts, send_peer, recv_from, key_weight, value_weight, hidden, queries, out_grad):
    rows, width = key_weight.shape
    blocks, group = lax.axis_size("fsdp"), lax.axis_size("dp")
    slots, tokens, _ = hidden.shape
    total, cols, span, chips = slots * tokens, 2 * width, 2 * rows, blocks // 2
    bf16 = jnp.bfloat16
    smem = pl.BlockSpec(memory_space=pltpu.SMEM)
    hbm = pl.BlockSpec(memory_space=pl.ANY)

    def buffer(*shape):
        return pltpu.VMEM(shape, bf16)

    return pl.pallas_call(
        main_kernel,
        name="main",
        out_shape=(
            jax.ShapeDtypeStruct(hidden.shape, bf16),
            jax.ShapeDtypeStruct((2, 2, 4, width // 8, span), bf16),
        ),
        in_specs=[smem, smem, smem, hbm, hbm, hbm, hbm, hbm],
        out_specs=(hbm, hbm),
        scratch_shapes=[
            buffer(blocks, rows, cols),
            buffer(*hidden.shape),
            buffer(*queries.shape),
            buffer(*out_grad.shape),
            pltpu.VMEM((total, cols), jnp.float32),
            buffer(total, cols),
            buffer(total, cols),
            buffer(group, tokens, cols),
            buffer(group, tokens, cols),
            buffer(total, cols),
            buffer(2, width, total),
            buffer(chips, width, span),
            buffer(chips, slots, tokens, span),
            buffer(chips, slots, tokens, span),
            buffer(2, width, 256),
            buffer(2, 2, width, 256),
            buffer(8, width // 8, 384),
            buffer(2, 8, width // 8, 384),
            buffer(4, width // 4, 384),
            buffer(2, 4, width // 4, 384),
            buffer(3, width // 2, 256),
            buffer(3, 2, width // 8, 384),
            buffer(3, 4, width // 16, 384),
            buffer(3, width // 8, 256),
            buffer(3, width // 16, 384),
            buffer(3, width // 16, 384),
            buffer(2, 2, 4, width // 8, span),
            pltpu.SemaphoreType.DMA((192,)),
            pltpu.SemaphoreType.DMA((192,)),
            pltpu.SemaphoreType.DMA((12,)),
        ],
        compiler_params=pltpu.CompilerParams(
            collective_id=0, has_side_effects=True, vmem_limit_bytes=62 << 20
        ),
        cost_estimate=pl.CostEstimate(
            flops=6 * total * blocks * rows * cols, bytes_accessed=22 << 20, transcendentals=0
        ),
    )(counts, send_peer, recv_from, key_weight, value_weight, hidden, queries, out_grad)


def finish_kernel(hg_in, pieces_in, hg_out, key_grad, value_grad, hg, pieces, sem):
    chunks = 8
    step = hg.shape[0] // chunks
    first = pltpu.make_async_copy(pieces_in, pieces, sem.at[2 * chunks])
    first.start()

    def chunk(i, src, dst, offset):
        at = pl.ds(i * step, step)
        return pltpu.make_async_copy(src.at[at], dst.at[at], sem.at[offset + i])

    for i in range(chunks):
        chunk(i, hg_in, hg, 0).start()
    first.wait()
    for i in range(chunks):
        chunk(i, hg_in, hg, 0).wait()
        chunk(i, hg, hg_out, chunks).start()
    core = lax.rem(lax.axis_index("fsdp"), 2)
    rows, width = key_grad.shape
    for t, out in enumerate((key_grad, value_grad)):
        left = pieces[t, :, :, :, :256].reshape(width, 256)
        upper = [pieces[t, l, z, :32, 256:] for z in range(4) for l in range(2)]
        lower = [pieces[t, l, z, 32:, 256:] for l in range(2) for z in range(4)]
        right = jnp.concatenate(upper + lower, axis=0)
        grads = jnp.concatenate([left, right], axis=1)
        grads = grads.astype(jnp.float32)
        out[...] = jnp.where(core == 0, grads[:, :rows], grads[:, rows:]).T
    for i in range(chunks):
        chunk(i, hg, hg_out, chunks).wait()


def finish(hidden_grad, pieces):
    rows, width = pieces.shape[-1] // 2, pieces.shape[1] * pieces.shape[2] * pieces.shape[3]
    vmem = pl.BlockSpec(memory_space=pltpu.VMEM)
    hbm = pl.BlockSpec(memory_space=pl.ANY)
    grad = jax.ShapeDtypeStruct((rows, width), jnp.float32)
    return pl.pallas_call(
        finish_kernel,
        name="finish",
        out_shape=(jax.ShapeDtypeStruct(hidden_grad.shape, hidden_grad.dtype), grad, grad),
        in_specs=[hbm, hbm],
        out_specs=(hbm, vmem, vmem),
        scratch_shapes=[
            pltpu.VMEM(hidden_grad.shape, hidden_grad.dtype),
            pltpu.VMEM(pieces.shape, pieces.dtype),
            pltpu.SemaphoreType.DMA((17,)),
        ],
        compiler_params=pltpu.CompilerParams(vmem_limit_bytes=60 << 20),
    )(hidden_grad, pieces)


def body(hidden, queries, out_grad, counts, send_peer, recv_from, key_weight, value_weight):
    hidden_grad, pieces = main_call(
        counts, send_peer, recv_from, key_weight, value_weight, hidden, queries, out_grad
    )
    return finish(hidden_grad, pieces)


def solution(mesh):
    return jax.shard_map(
        body,
        mesh=mesh,
        in_specs=(
            P(("dp", "fsdp"), None, None),
            P(("dp", "fsdp"), None, None),
            P(("dp", "fsdp"), None, None),
            P(("dp", "fsdp")),
            P(("dp", "fsdp")),
            P(("dp", "fsdp")),
            P("fsdp", None),
            P("fsdp", None),
        ),
        out_specs=(P(("dp", "fsdp"), None, None), P("fsdp", None), P("fsdp", None)),
        check_vma=False,
    )
```
